32 devices in a mesh: ccd: 8 (over y, x, core), amp: 4 (over z).
Axes of the slice: x: 2, y: 2, z: 4, core: 2. Of those that a mesh axis runs over, the one named last changes fastest.
Arguments:
- science: float32 [8, 512, 4096], P('ccd', 'amp'), may hold values from -6 to 6
- patches: float32 [8, 4, 4, 256, 256], P('ccd', 'amp'), may hold values from -6 to 6
- coeffs: float32 [8, 40, 6], P('ccd'), may hold values from -0.9 to 0.9
- tile_owner: int32 [8, 4, 32, 1], replicated, may hold values from 0 to 7; in each aligned block of 32 rows (0 to 31, 32 to 63, ..., all dimensions but the last counted through in order) at most 8 rows name the same one
- tile_patch: int32 [8, 4, 32], replicated, may hold values from 0 to 3
- tile_offset: int32 [8, 4, 32, 2], replicated, may hold values from 0 to 128
Outputs:
- difference: float32 [8, 512, 4096], P('ccd', 'amp')
The draws below stay inside these ranges and needn't reach their ends.
Inputs may be any that keep to these rules, and one draw needn't show every extreme that they name: `tile_owner`: among the 32 tiles of one strip, at most 8 name the same owner.
All inputs are finite; a program needn't handle non-finite values.
Results may differ from the reference program's by a relative error of at most 0.0031.
Values may be sent and summed in bfloat16 or wider, within the bound.
A program may use at most 128 MiB of HBM per device.

```python
import math
import jax
import jax.numpy as jnp
import numpy as np
from jax import lax

W = 4096
TS = 128
PS = 256
PATCH_DEV = 4
HALF = 10
K = 40
NPOLY = 6
TROWS = 1
ROWS_DEV = 128
TILES_DEV = 32
CAP = 8
NROWS = 512
N_CCD = 8
N_AMP = 4


def draw_patches(key, part):
    key = jax.random.fold_in(key, 11)
    patch_shape = (N_CCD, N_AMP, PATCH_DEV, PS, PS)
    return jnp.clip(jax.random.normal(key, patch_shape, jnp.float32), -6.0, 6.0)


def draw_coeffs(key, part):
    key = jax.random.fold_in(key, 23)
    coeff_shape = (N_CCD, K, NPOLY)
    return jnp.clip(0.15 * jax.random.normal(key, coeff_shape, jnp.float32), -0.9, 0.9)


def touch_ends(values, key, low, top_value):
    longest = values.shape.index(max(values.shape))
    spots = []
    for shift in (0, 1):
        where = [jax.random.randint(jax.random.fold_in(key, axis), (), 0, length) for axis, length in enumerate(values.shape)]
        where[longest] = (where[longest] + shift) % values.shape[longest]
        spots.append(tuple(where))
    return values.at[spots[0]].set(low).at[spots[1]].set(top_value)


def level_of(own_key, dims, shards, low, high):
    def one(position, blocks):
        heights = jax.random.uniform(jax.random.fold_in(jax.random.fold_in(own_key, 6), position), (blocks,), jnp.float32, low / len(shards), high / len(shards))
        return jnp.repeat(jnp.exp(heights), dims[position] // blocks).reshape((-1,) + (1,) * (len(dims) - position - 1))

    level = one(*shards[0])
    for cut in shards[1:]:
        level = level * one(*cut)
    return level


def routed_block(own_key, own, number, rows, number_of, top, most, slope):
    sequence = jax.random.permutation(own_key, number_of)
    packed, ordinary = portions_of(number_of, rows * top, most, slope, True), portions_of(number_of, rows * top, most, slope, False)
    places = jnp.arange(number_of)

    def named(tallies, offset_by):
        used = int((tallies > 0).sum())
        fixed = max(1, used // 4)
        passed = fixed + (places - fixed + offset_by * (used - fixed)) % max(1, number_of - fixed)
        return jnp.zeros((number_of,), jnp.int32).at[sequence[jnp.where(places < fixed, places, passed)]].set(jnp.asarray(tallies, jnp.int32))

    tallies = jnp.where(number % 4 == 0, named(packed, number // 4), named(ordinary, number - number // 4 - 1))
    mixed = jax.random.permutation(jax.random.fold_in(own, 3), number_of)
    donor, receiver = mixed[0:number_of // 2 * 2:2], mixed[1:number_of // 2 * 2:2]
    room = jnp.minimum(tallies[donor] - 1, most - tallies[receiver]) // 2
    room = jnp.where((donor == sequence[0]) | (receiver == sequence[0]) | (tallies[receiver] == 0), 0, jnp.maximum(room, 0))
    passed = jax.random.randint(jax.random.fold_in(own, 4), (number_of // 2,), 0, 1 << 20) % (room + 1)
    tallies = tallies.at[donor].add(-passed).at[receiver].add(passed)
    items = jnp.searchsorted(jnp.cumsum(tallies), jnp.arange(rows * top), side="right").astype(jnp.int32)
    grid = items.reshape(top, rows).T
    grid = grid[jax.random.permutation(jax.random.fold_in(own, 1), rows)]
    offset_by = jax.random.randint(jax.random.fold_in(own, 2), (rows, 1), 0, top)
    return jnp.take_along_axis(grid, (jnp.arange(top)[None, :] + offset_by) % top, axis=1)


def portions_of(count, total, bound, skew, full):
    loads = [(1 << 20) // math.isqrt(grade ** skew) + 1 for grade in range(1, count + 1)]
    largest = bound if full else min(bound, max(-(-total // count), total * loads[0] // sum(loads)))
    least = 1 if total - largest >= count - 1 else 0
    holding, rest = [largest] + [least] * (count - 1), total - largest - least * (count - 1)
    while rest > 0:
        free = [i for i in range(1, count) if holding[i] < largest] or [i for i in range(1, count) if holding[i] < bound]
        pool, left = sum([loads[i] for i in free]), rest
        for i in free:
            extra = min(bound - holding[i], max(1, left * loads[i] // pool), rest)
            holding[i] = holding[i] + extra
            rest = rest - extra
    return np.array(holding)


def centred(rng, shape, width, reach, cuts=(), kind=jnp.bfloat16):
    result = width * jax.random.normal(rng, shape, jnp.float32)
    if cuts:
        result = result * level_of(rng, shape, cuts, -0.22, 0.18)
    return jnp.clip(result, -reach, reach).astype(kind)


def setup_inputs(seed: int = 0) -> dict:
    key_of = jax.random.split(jax.random.key(seed), 7)
    science = centred(key_of[0], (N_CCD, NROWS, W), 1.0, 6.0, ((0, 8), (1, 4)), jnp.float32)
    patches = draw_patches(jax.random.fold_in(key_of[6], 71), 0)
    coeffs = draw_coeffs(jax.random.fold_in(key_of[6], 71), 0)
    tile_owner_keys = jax.random.split(jax.random.fold_in(key_of[3], 1), N_CCD * N_AMP * TILES_DEV // TILES_DEV)
    tile_owner_turns = jax.random.permutation(jax.random.fold_in(key_of[3], 3), N_CCD * N_AMP * TILES_DEV // TILES_DEV)
    tile_owner = jax.vmap(lambda own, number: routed_block(jax.random.fold_in(key_of[3], 2), own, number, TILES_DEV, N_CCD, 1, CAP, 2))(tile_owner_keys, tile_owner_turns).reshape((N_CCD, N_AMP, TILES_DEV, 1))
    tile_patch = touch_ends(jax.random.randint(key_of[4], (N_CCD, N_AMP, TILES_DEV), 0, PATCH_DEV), jax.random.fold_in(key_of[4], 1), 0, PATCH_DEV - 1).astype(jnp.int32)
    tile_offset = touch_ends(jax.random.randint(key_of[5], (N_CCD, N_AMP, TILES_DEV, 2), 0, PS - TS + 1), jax.random.fold_in(key_of[5], 1), 0, PS - TS).astype(jnp.int32)
    return {"science": science, "patches": patches, "coeffs": coeffs, "tile_owner": tile_owner, "tile_patch": tile_patch, "tile_offset": tile_offset}


gauss_widths = (1.0, 2.0, 4.0)
poly_degrees = (4, 4, 3)


def factor_table(half):
    offsets = jnp.arange(-half, half + 1).astype(jnp.float32)
    shapes = []
    for sigma_px, degree in zip(gauss_widths, poly_degrees):
        for exponent in range(degree + 1):
            profile = jnp.exp(-offsets * offsets / (2.0 * sigma_px * sigma_px)) * (offsets / half) ** exponent
            shapes.append(profile / jnp.sum(jnp.abs(profile)))
    return jnp.stack(shapes).astype(jnp.bfloat16)


def basis_groups():
    grouped_pairs = []
    first_factor = 0
    for degree in poly_degrees:
        members = []
        for across_pow in range(degree + 1):
            for down_pow in range(degree + 1 - across_pow):
                members.append((first_factor + across_pow, first_factor + down_pow))
        grouped_pairs.append(members)
        first_factor = first_factor + degree + 1
    return grouped_pairs


def across_matrices(factors, half):
    column = jnp.arange(256)[:, None]
    output = jnp.arange(128)[None, :]
    lag_cols = column - 64 - output
    tap_offsets = jnp.arange(-half, half + 1)
    select = (lag_cols[:, :, None] == tap_offsets[None, None, :]).astype(jnp.float32)
    mats = jnp.einsum('cqt,ht->hcq', select, factors.astype(jnp.float32), precision=lax.Precision.HIGHEST)
    return mats.astype(jnp.bfloat16)


def down_matrices(factors, half, strip_rows):
    target = jnp.arange(strip_rows)[:, None]
    source = jnp.arange(strip_rows + 2 * half)[None, :]
    lag_rows = source - half - target
    tap_offsets = jnp.arange(-half, half + 1)
    select = (lag_rows[:, :, None] == tap_offsets[None, None, :]).astype(jnp.float32)
    mats = jnp.einsum('yrt,ht->hyr', select, factors.astype(jnp.float32), precision=lax.Precision.HIGHEST)
    return mats.astype(jnp.bfloat16)


def strip_model(padded, coeff_rows, row_first, total_rows, across_mats, down_mats):
    padded_rows, columns = padded.shape
    strip_rows = padded_rows - 2 * HALF
    block_count = columns // 128
    blocks = padded.reshape(padded_rows, block_count, 128)
    empty_rim = jnp.zeros((padded_rows, 1, 64), padded.dtype)
    left_rim = jnp.concatenate([empty_rim, blocks[:, :-1, 64:]], axis=1)
    right_rim = jnp.concatenate([blocks[:, 1:, :64], empty_rim], axis=1)
    window = jnp.concatenate([left_rim, blocks, right_rim], axis=2)
    per_group = math.gcd(block_count, 8)
    group_count = block_count // per_group
    grouped = window.reshape(padded_rows, group_count, per_group, 256).transpose(1, 0, 2, 3)
    ycoord = (2.0 * (row_first + jnp.arange(strip_rows)).astype(jnp.float32) + 1.0) / total_rows - 1.0
    group_cols = per_group * 128

    def one_group(group_inputs):
        group_window, group_index = group_inputs
        xcoord = (2.0 * (group_index * group_cols + jnp.arange(group_cols)).astype(jnp.float32) + 1.0) / columns - 1.0
        xgrid = jnp.broadcast_to(xcoord[None, :], (strip_rows, group_cols))
        ygrid = jnp.broadcast_to(ycoord[:, None], (strip_rows, group_cols))
        poly_terms = jnp.stack([jnp.ones_like(xgrid), xgrid, ygrid, xgrid * xgrid, xgrid * ygrid, ygrid * ygrid])
        across_all = jnp.einsum('rbc,hcq->hrbq', group_window.astype(jnp.float32), across_mats.astype(jnp.float32), precision=lax.Precision.HIGHEST)
        across_all = across_all.astype(jnp.bfloat16).reshape(across_mats.shape[0], padded_rows, group_cols)
        psf_part = jnp.zeros((strip_rows, group_cols), jnp.float32)
        basis_first = 0
        for members in basis_groups():
            across_index = np.array([member[0] for member in members], dtype=np.int32)
            down_index = np.array([member[1] for member in members], dtype=np.int32)
            inputs = across_all[across_index].astype(jnp.float32)
            kernels = down_mats[down_index].astype(jnp.float32)
            convolved = jnp.einsum('kyr,krx->kyx', kernels, inputs, precision=lax.Precision.HIGHEST)
            weights = coeff_rows[basis_first:basis_first + len(members)]
            folded = jnp.einsum('km,kyx->myx', weights, convolved, precision=lax.Precision.HIGHEST)
            psf_part = psf_part + jnp.sum(folded * poly_terms, axis=0)
            basis_first = basis_first + len(members)
        return psf_part

    parts = lax.map(one_group, (grouped, jnp.arange(group_count, dtype=jnp.int32)))
    return parts.transpose(1, 0, 2).reshape(strip_rows, columns)


def assemble(patches, tile_owner, tile_patch, tile_offset):
    store_bf = patches.astype(jnp.bfloat16)
    amp_ids = jnp.broadcast_to(jnp.arange(N_AMP, dtype=jnp.int32)[None, :, None], (N_CCD, N_AMP, TILES_DEV))

    def crop(owner_id, amp_id, patch_id, row_shift, col_shift):
        start = (owner_id.astype(jnp.int32), amp_id.astype(jnp.int32), patch_id.astype(jnp.int32), row_shift.astype(jnp.int32), col_shift.astype(jnp.int32))
        return lax.dynamic_slice(store_bf, start, (1, 1, 1, TS, TS))[0, 0, 0]

    tile_stack = jax.vmap(crop)(tile_owner[..., 0].reshape(-1), amp_ids.reshape(-1), tile_patch.reshape(-1), tile_offset[..., 0].reshape(-1), tile_offset[..., 1].reshape(-1))
    tile_stack = tile_stack.reshape(N_CCD, N_AMP, TROWS, W // TS, TS, TS).transpose(0, 1, 2, 4, 3, 5)
    return tile_stack.reshape(N_CCD, NROWS, W)


def reference(science, patches, coeffs, tile_owner, tile_patch, tile_offset):
    template = assemble(patches, tile_owner, tile_patch, tile_offset)
    padded = jnp.pad(template, ((0, 0), (HALF, HALF), (0, 0)))
    factors = factor_table(HALF)
    across_mats = across_matrices(factors, HALF)
    down_mats = down_matrices(factors, HALF, ROWS_DEV)

    def one_ccd(ccd_inputs):
        padded_ccd, science_ccd, coeff_ccd = ccd_inputs

        def one_amp(amp_id):
            row_first = amp_id * ROWS_DEV
            strip_padded = lax.dynamic_slice_in_dim(padded_ccd, row_first, ROWS_DEV + 2 * HALF, 0)
            strip_science = lax.dynamic_slice_in_dim(science_ccd, row_first, ROWS_DEV, 0)
            return strip_science - strip_model(strip_padded, coeff_ccd, row_first, NROWS, across_mats, down_mats)

        strips = lax.map(one_amp, jnp.arange(N_AMP, dtype=jnp.int32))
        return strips.reshape(NROWS, W)

    return lax.map(one_ccd, (padded, science, coeffs))
```

```python
import functools

import jax
import jax.numpy as jnp
import ml_dtypes
import numpy as np
from jax import lax
from jax.experimental import pallas as pl
from jax.experimental.pallas import tpu as pltpu
from jax.sharding import PartitionSpec as P

TS = 128
HALF = 10
RIM = 16
WINDOW = 2 * TS
VMEM_BYTES = 48 * 2**20

gauss_widths = (1.0, 2.0, 4.0)
poly_degrees = (4, 4, 3)
poly_powers = ((0, 0), (1, 0), (0, 1), (2, 0), (1, 1), (0, 2))
QMAX = max(poly_degrees) + 1


def factor_table():
    offsets = np.arange(-HALF, HALF + 1).astype(np.float64)
    shapes = []
    for sigma_px, degree in zip(gauss_widths, poly_degrees):
        for exponent in range(degree + 1):
            profile = np.exp(-offsets * offsets / (2.0 * sigma_px * sigma_px))
            profile = profile * (offsets / HALF) ** exponent
            shapes.append(profile / np.sum(np.abs(profile)))
    return np.stack(shapes).astype(np.float32).astype(ml_dtypes.bfloat16).astype(np.float32)


def across_pairs():
    return [(s, p) for s, degree in enumerate(poly_degrees) for p in range(degree + 1)]


def banded(taps, lags):
    inside = np.abs(lags) <= HALF
    return np.where(inside, taps[np.clip(lags + HALF, 0, 2 * HALF)], 0.0)


def across_matrix():
    factors = factor_table()
    lags = np.arange(WINDOW)[:, None] - TS // 2 - np.arange(TS)[None, :]
    return np.concatenate([banded(f, lags) for f in factors], axis=1).astype(ml_dtypes.bfloat16)


def down_factors(lags):
    factors = factor_table()
    first = np.concatenate([[0], np.cumsum([d + 1 for d in poly_degrees])])
    out = []
    for q in range(QMAX):
        row = []
        for s, p in across_pairs():
            if q <= poly_degrees[s]:
                row.append(banded(factors[first[s] + q], lags))
            else:
                row.append(np.zeros(lags.shape))
        out.append(np.concatenate(row, axis=1))
    return np.stack(out).astype(ml_dtypes.bfloat16)


def basis_select():
    pairs = across_pairs()
    select = np.zeros((QMAX, len(pairs), sum(d + 1 - p for d in poly_degrees for p in range(d + 1))))
    k = 0
    for h, (s, p) in enumerate(pairs):
        for q in range(poly_degrees[s] + 1 - p):
            select[q, h, k] = 1.0
            k += 1
    return select.astype(np.float32)


def weights_kernel(c_ref, y_ref, d_ref, out_ref):
    yh = y_ref[...]
    factors = [d_ref[q].astype(jnp.float32) for q in range(QMAX)]
    for a in range(3):
        total = None
        for m, (xp, yp) in enumerate(poly_powers):
            if xp != a:
                continue
            term = None
            for q in range(QMAX):
                part = c_ref[m * QMAX + q : m * QMAX + q + 1, :] * factors[q]
                term = part if term is None else term + part
            for _ in range(yp):
                term = term * yh
            total = term if total is None else total + term
        out_ref[a] = total.astype(out_ref.dtype)


def build_weights(coeff_lanes, ycol, down, lanes):
    rows, width = down.shape[1:]
    return pl.pallas_call(
        weights_kernel,
        grid=(width // lanes,),
        in_specs=[
            pl.BlockSpec((coeff_lanes.shape[0], lanes), lambda i: (0, i)),
            pl.BlockSpec((rows, 1), lambda i: (0, 0)),
            pl.BlockSpec((QMAX, rows, lanes), lambda i: (0, 0, i)),
        ],
        out_specs=pl.BlockSpec((3, rows, lanes), lambda i: (0, 0, i)),
        out_shape=jax.ShapeDtypeStruct((3, rows, width), jnp.bfloat16),
        compiler_params=pltpu.CompilerParams(vmem_limit_bytes=VMEM_BYTES),
        cost_estimate=pl.CostEstimate(
            flops=40 * 2 * rows * width, bytes_accessed=16 * rows * width, transcendentals=0
        ),
    )(coeff_lanes, ycol, down)


def crop_kernel(per_step, owner, patch, row_shift, col_shift, *refs):
    patch_refs, out_ref, carry = refs[:per_step], refs[per_step], refs[per_step + 1]
    step = pl.program_id(0)

    @pl.when(step == 0)
    def _():
        carry[...] = jnp.zeros_like(carry)

    row_lag = lax.broadcasted_iota(jnp.int32, (TS, 2 * TS), 1) - lax.broadcasted_iota(
        jnp.int32, (TS, 2 * TS), 0
    )
    col_lag = lax.broadcasted_iota(jnp.int32, (2 * TS, 2 * TS), 0) - lax.broadcasted_iota(
        jnp.int32, (2 * TS, 2 * TS), 1
    )
    column = lax.broadcasted_iota(jnp.int32, (2 * TS, 2 * TS), 1)
    held = (column >= TS // 2) & (column < TS // 2 + TS)
    col_lag = jnp.where(held, col_lag + TS // 2, -1)
    before = carry[...]
    for j in range(per_step):
        t = step * per_step + j
        pick_rows = (row_lag == row_shift[t]).astype(jnp.float32).astype(jnp.bfloat16)
        pick_cols = (col_lag == col_shift[t]).astype(jnp.float32).astype(jnp.bfloat16)
        rows = jnp.dot(pick_rows, patch_refs[j][0, 0, 0], preferred_element_type=jnp.float32)
        wide = jnp.dot(
            rows.astype(jnp.bfloat16), pick_cols, preferred_element_type=jnp.float32
        ).astype(jnp.bfloat16)
        first = pl.multiple_of(t * TS, TS)
        out_ref[:, pl.ds(first, TS)] = before + wide[:, :TS]
        before = wide[:, TS:]
    carry[...] = before

    @pl.when(step == pl.num_programs(0) - 1)
    def _():
        out_ref[:, out_ref.shape[1] - TS :] = before


def crop(piece, owner, patch, row_shift, col_shift):
    tiles = owner.shape[0]
    per_step = 8

    def block(j):
        return pl.BlockSpec(
            (1, 1, 1, 2 * TS, 2 * TS),
            lambda i, own, pat, dy, dx: (own[i * per_step + j], 0, pat[i * per_step + j], 0, 0),
        )

    width = (tiles + 1) * TS
    return pl.pallas_call(
        functools.partial(crop_kernel, per_step),
        grid_spec=pltpu.PrefetchScalarGridSpec(
            num_scalar_prefetch=4,
            grid=(tiles // per_step,),
            in_specs=[block(j) for j in range(per_step)],
            out_specs=pl.BlockSpec((TS, width), lambda i, *_: (0, 0)),
            scratch_shapes=[pltpu.VMEM((TS, TS), jnp.bfloat16)],
        ),
        out_shape=jax.ShapeDtypeStruct((TS, width), jnp.bfloat16),
        compiler_params=pltpu.CompilerParams(vmem_limit_bytes=VMEM_BYTES),
        cost_estimate=pl.CostEstimate(
            flops=tiles * 2 * TS * 8 * TS * TS, bytes_accessed=5 * 2**20, transcendentals=0
        ),
    )(owner, patch, row_shift, col_shift, *([piece] * per_step))


def apply_factors(windows, across_ref, weights, spread, columns, first_column):
    rows = windows[0].shape[0]
    stacked = jnp.concatenate(windows, axis=0)
    for pair in range(across_ref.shape[1] // WINDOW):
        result = jnp.dot(
            stacked,
            across_ref[:, pair * WINDOW : (pair + 1) * WINDOW],
            preferred_element_type=jnp.float32,
        ).astype(jnp.bfloat16)
        for b in range(len(windows)):
            for half in range(2):
                h = 2 * pair + half
                spread[h * rows : (h + 1) * rows, b * TS : (b + 1) * TS] = result[
                    b * rows : (b + 1) * rows, half * TS : (half + 1) * TS
                ]
    folded = jnp.dot(weights, spread[...], preferred_element_type=jnp.float32)
    out_rows = weights.shape[0] // 3
    width = len(windows) * TS
    position = first_column + lax.broadcasted_iota(jnp.int32, (1, width), 1)
    xh = (2.0 * position.astype(jnp.float32) + 1.0) / columns - 1.0
    return folded[:out_rows] + xh * (
        folded[out_rows : 2 * out_rows] + xh * folded[2 * out_rows :]
    )


def centre_kernel(columns, template_ref, across_ref, weight_ref, science_ref, out_ref, spread):
    width = out_ref.shape[1]
    first = pl.program_id(0) * width
    windows = [
        template_ref[:, pl.ds(pl.multiple_of(first + b * TS, TS), WINDOW)]
        for b in range(width // TS)
    ]
    weights = weight_ref[...].reshape(-1, weight_ref.shape[2])
    psf = apply_factors(windows, across_ref, weights, spread, columns, first)
    out_ref[...] = science_ref[...] - psf


def centre(template, across, weights, science, width):
    rows, columns = science.shape
    return pl.pallas_call(
        functools.partial(centre_kernel, columns),
        grid=(columns // width,),
        in_specs=[
            pl.BlockSpec(template.shape, lambda i: (0, 0)),
            pl.BlockSpec(across.shape, lambda i: (0, 0)),
            pl.BlockSpec(weights.shape, lambda i: (0, 0, 0)),
            pl.BlockSpec((rows, width), lambda i: (0, i)),
        ],
        out_specs=pl.BlockSpec((rows, width), lambda i: (0, i)),
        out_shape=jax.ShapeDtypeStruct(science.shape, jnp.float32),
        scratch_shapes=[pltpu.VMEM((weights.shape[2], width), jnp.bfloat16)],
        compiler_params=pltpu.CompilerParams(vmem_limit_bytes=VMEM_BYTES),
        cost_estimate=pl.CostEstimate(
            flops=2 * columns * weights.shape[2] * (3 * rows + WINDOW),
            bytes_accessed=8 * rows * columns + 4 * 2**20,
            transcendentals=0,
        ),
    )(template, across, weights, science)


def rim_kernel(columns, top_ref, low_ref, across_ref, weight_ref, held_ref, out_ref, spread):
    width = out_ref.shape[1]
    first = pl.program_id(1) * width
    is_top = pl.program_id(0) == 0
    windows = []
    for b in range(width // TS):
        where = pl.ds(pl.multiple_of(first + b * TS, TS), WINDOW)
        windows.append(jnp.where(is_top, top_ref[:, where], low_ref[:, where]))
    weights = weight_ref[...].reshape(-1, weight_ref.shape[2])
    psf = apply_factors(windows, across_ref, weights, spread, columns, first)
    out_ref[...] = held_ref[...] - psf


def rims(top, low, across, weights, held, width):
    rows, columns = held.shape
    last = rows // RIM - 1
    return pl.pallas_call(
        functools.partial(rim_kernel, columns),
        grid=(2, columns // width),
        in_specs=[
            pl.BlockSpec(top.shape, lambda v, i: (0, 0)),
            pl.BlockSpec(low.shape, lambda v, i: (0, 0)),
            pl.BlockSpec(across.shape, lambda v, i: (0, 0)),
            pl.BlockSpec((3, RIM, weights.shape[2]), lambda v, i: (0, v, 0)),
            pl.BlockSpec((RIM, width), lambda v, i: (v * last, i)),
        ],
        out_specs=pl.BlockSpec((RIM, width), lambda v, i: (v * last, i)),
        out_shape=jax.ShapeDtypeStruct(held.shape, jnp.float32),
        scratch_shapes=[pltpu.VMEM((weights.shape[2], width), jnp.bfloat16)],
        input_output_aliases={4: 0},
        compiler_params=pltpu.CompilerParams(vmem_limit_bytes=VMEM_BYTES),
        cost_estimate=pl.CostEstimate(
            flops=4 * columns * weights.shape[2] * (3 * RIM + WINDOW),
            bytes_accessed=2**20,
            transcendentals=0,
        ),
    )(top, low, across, weights, held)


def per_device(science, patches, coeffs, tile_owner, tile_patch, tile_offset):
    ccd_id = lax.axis_index("ccd")
    amp_id = lax.axis_index("amp")
    amp_count = lax.axis_size("amp")
    strip_rows, columns = science.shape[1:]

    piece = lax.all_gather(patches.astype(jnp.bfloat16), "ccd", axis=0, tiled=True)

    owner = tile_owner[ccd_id, amp_id, :, 0]
    patch = tile_patch[ccd_id, amp_id]
    row_shift = tile_offset[ccd_id, amp_id, :, 0]
    col_shift = tile_offset[ccd_id, amp_id, :, 1]

    across = jnp.asarray(across_matrix())
    row = np.arange(strip_rows)
    centre_down = down_factors(row[None, :] - row[:, None])
    rim_row = np.arange(RIM)
    top_lags = (rim_row[None, :] - RIM) - rim_row[:, None]
    low_lags = (rim_row[None, :] + RIM) - rim_row[:, None]
    rim_down = np.concatenate([down_factors(top_lags), down_factors(low_lags)], axis=1)
    select = jnp.asarray(basis_select())
    coeff_table = jnp.einsum("qhk,km->mqh", select, coeffs[0], precision=lax.Precision.HIGHEST)
    coeff_table = coeff_table.reshape(-1, coeff_table.shape[2])
    ycoord = (
        2.0 * (amp_id * strip_rows + jnp.arange(strip_rows)).astype(jnp.float32) + 1.0
    ) / (amp_count * strip_rows) - 1.0
    ycol = ycoord[:, None]
    centre_weights = build_weights(
        jnp.repeat(coeff_table, strip_rows, axis=1), ycol, jnp.asarray(centre_down), 2 * strip_rows
    )
    rim_weights = build_weights(
        jnp.repeat(coeff_table, RIM, axis=1),
        jnp.concatenate([ycol[:RIM], ycol[-RIM:]], axis=0),
        jnp.asarray(rim_down),
        rim_down.shape[2],
    )

    template = crop(piece, owner, patch, row_shift, col_shift)
    forward = [(i, i + 1) for i in range(amp_count - 1)]
    backward = [(i + 1, i) for i in range(amp_count - 1)]
    top = lax.ppermute(template[-RIM:], "amp", forward)
    low = lax.ppermute(template[:RIM], "amp", backward)
    inner = centre(template, across, centre_weights, science[0], 8 * TS)
    return rims(top, low, across, rim_weights, inner, 16 * TS)[None]


def solution(mesh):
    placed = (
        P("ccd", "amp", None),
        P("ccd", "amp", None, None, None),
        P("ccd", None, None),
        P(),
        P(),
        P(),
    )
    return jax.shard_map(
        per_device, mesh=mesh, in_specs=placed, out_specs=P("ccd", "amp", None), check_vma=False
    )
```

```python
import functools

import jax
import jax.numpy as jnp
import ml_dtypes
import numpy as np
from jax import lax
from jax.experimental import pallas as pl
from jax.experimental.pallas import tpu as pltpu
from jax.sharding import PartitionSpec as P

TS = 128
HALF = 10
RIM = 16
WINDOW = 2 * TS
VMEM_BYTES = 48 * 2**20

gauss_widths = (1.0, 2.0, 4.0)
poly_degrees = (4, 4, 3)
poly_powers = ((0, 0), (1, 0), (0, 1), (2, 0), (1, 1), (0, 2))


def factor_table():
    offsets = np.arange(-HALF, HALF + 1).astype(np.float64)
    shapes = []
    for sigma_px, degree in zip(gauss_widths, poly_degrees):
        for exponent in range(degree + 1):
            profile = np.exp(-offsets * offsets / (2.0 * sigma_px * sigma_px))
            profile = profile * (offsets / HALF) ** exponent
            shapes.append(profile / np.sum(np.abs(profile)))
    return np.stack(shapes).astype(np.float32).astype(ml_dtypes.bfloat16).astype(np.float32)


def across_pairs():
    return [(s, p) for s, degree in enumerate(poly_degrees) for p in range(degree + 1)]


def banded(taps, lags):
    inside = np.abs(lags) <= HALF
    return np.where(inside, taps[np.clip(lags + HALF, 0, 2 * HALF)], 0.0)


def across_matrix():
    factors = factor_table()
    lags = np.arange(WINDOW)[:, None] - TS // 2 - np.arange(TS)[None, :]
    return np.concatenate([banded(f, lags) for f in factors], axis=1).astype(ml_dtypes.bfloat16)


def factor_firsts():
    return [int(f) for f in np.concatenate([[0], np.cumsum([d + 1 for d in poly_degrees])])]


def down_factors(lags, lanes):
    bands = np.stack([banded(f, lags) for f in factor_table()])
    return np.pad(bands, ((0, 0), (0, 0), (0, lanes - lags.shape[1]))).astype(ml_dtypes.bfloat16)


def lane_packing():
    pack = np.zeros((TS // RIM, TS, TS))
    for g in range(TS // RIM):
        for r in range(RIM):
            pack[g, r, g * RIM + r] = 1.0
    return pack.reshape(-1, TS).astype(ml_dtypes.bfloat16)


def fold_weights(coeff_ref, yh, down_ref, out_ref):
    firsts = factor_firsts()
    k = 0
    for h, (s, p) in enumerate(across_pairs()):
        count = poly_degrees[s] + 1 - p
        factors = [down_ref[firsts[s] + q].astype(jnp.float32) for q in range(count)]
        terms = [
            sum(coeff_ref[k + q, m] * factors[q] for q in range(count))
            for m in range(len(poly_powers))
        ]
        k += count
        where = slice(h * TS, (h + 1) * TS)
        out_ref[0, :, where] = (terms[0] + yh * (terms[2] + yh * terms[5])).astype(jnp.bfloat16)
        out_ref[1, :, where] = (terms[1] + yh * terms[4]).astype(jnp.bfloat16)
        out_ref[2, :, where] = terms[3].astype(jnp.bfloat16)


def gather_kernel(
    owners,
    amps,
    owner,
    patch,
    row_shift,
    col_shift,
    coeff_ref,
    patches_ref,
    down_ref,
    rim_down_ref,
    pack_ref,
    template_ref,
    top_ref,
    low_ref,
    weight_ref,
    rim_weight_ref,
    store,
    rim_wide,
    top_land,
    low_land,
    direct_send,
    direct_recv,
    pass_send,
    pass_recv,
    own_send,
    own_recv,
    rim_send,
    rim_recv,
):
    mine = lax.axis_index("ccd")
    amp = lax.axis_index("amp")
    core = lax.rem(mine, 2)
    chip = lax.div(mine, 2)
    sibling = chip * 2 + 1 - core
    chips = owners // 2
    half = patches_ref.shape[0] // 2

    barrier = pltpu.get_barrier_semaphore()
    for step in range(1, owners):
        pl.semaphore_signal(
            barrier,
            inc=1,
            device_id=(lax.rem(mine + step, owners), amp),
            device_id_type=pl.DeviceIdType.MESH,
        )
    for step in (1, amps - 1):
        pl.semaphore_signal(
            barrier,
            inc=1,
            device_id=(mine, lax.rem(amp + step, amps)),
            device_id_type=pl.DeviceIdType.MESH,
        )
    store[mine] = patches_ref[...].astype(jnp.bfloat16)
    pl.semaphore_wait(barrier, owners - 1 + 2)

    def halves(of, which):
        return store.at[of, pl.ds(which * half, half)]

    def move(ref, send_sem, recv_sem, device):
        return pltpu.make_async_remote_copy(
            src_ref=ref,
            dst_ref=ref,
            send_sem=send_sem,
            recv_sem=recv_sem,
            device_id=device,
            device_id_type=pl.DeviceIdType.MESH,
        )

    sent = []
    for step in range(1, chips):
        target = lax.rem(chip + step, chips) * 2
        for j in range(2):
            copy = move(
                halves(mine, j),
                direct_send.at[step - 1, j],
                direct_recv.at[step - 1, core],
                (target + j, amp),
            )
            copy.start()
            sent.append(copy)
    own = move(store.at[mine], own_send, own_recv, (sibling, amp))
    own.start()

    rows = down_ref.shape[1]
    row = amp * rows + lax.broadcasted_iota(jnp.int32, (rows, 1), 0)
    yh = (2.0 * row.astype(jnp.float32) + 1.0) / (amps * rows) - 1.0
    fold_weights(coeff_ref, yh, down_ref, weight_ref)
    edge = lax.broadcasted_iota(jnp.int32, (2 * RIM, 1), 0)
    edge = amp * rows + jnp.where(edge < RIM, edge, rows - 2 * RIM + edge)
    yh = (2.0 * edge.astype(jnp.float32) + 1.0) / (amps * rows) - 1.0
    fold_weights(coeff_ref, yh, rim_down_ref, rim_wide)
    wide = rim_wide[...].reshape(3 * 2 * RIM, rim_wide.shape[2])
    group = pack_ref.shape[0]
    for g in range(rim_weight_ref.shape[2] // TS):
        part = wide[:, g * group : (g + 1) * group]
        packed = jnp.dot(part, pack_ref[: part.shape[1]], preferred_element_type=jnp.float32)
        rim_weight_ref[:, :, g * TS : (g + 1) * TS] = packed.astype(jnp.bfloat16).reshape(
            3, 2 * RIM, TS
        )

    for step in range(1, chips):
        source = lax.rem(chip + chips - step, chips) * 2
        for k in range(2):
            arrived = halves(source + k, core)
            move(
                arrived, direct_send.at[step - 1, k], direct_recv.at[step - 1, k], (sibling, amp)
            ).wait_recv()
            onward = move(
                arrived, pass_send.at[step - 1, k], pass_recv.at[step - 1, k], (sibling, amp)
            )
            onward.start()
            sent.append(onward)
    move(store.at[sibling], own_send, own_recv, (sibling, amp)).wait_recv()
    for step in range(1, chips):
        source = lax.rem(chip + chips - step, chips) * 2
        for k in range(2):
            move(
                halves(source + k, 1 - core),
                pass_send.at[step - 1, k],
                pass_recv.at[step - 1, k],
                (sibling, amp),
            ).wait_recv()

    row_lag = lax.broadcasted_iota(jnp.int32, (TS, 2 * TS), 1) - lax.broadcasted_iota(
        jnp.int32, (TS, 2 * TS), 0
    )
    col_lag = lax.broadcasted_iota(jnp.int32, (2 * TS, 2 * TS), 0) - lax.broadcasted_iota(
        jnp.int32, (2 * TS, 2 * TS), 1
    )
    column = lax.broadcasted_iota(jnp.int32, (2 * TS, 2 * TS), 1)
    held = (column >= TS // 2) & (column < TS // 2 + TS)
    col_lag = jnp.where(held, col_lag + TS // 2, -1)
    tiles = owner.shape[0]
    per_step = 8

    def cut(step, before):
        for j in range(per_step):
            t = step * per_step + j
            pick_rows = (row_lag == row_shift[t]).astype(jnp.float32).astype(jnp.bfloat16)
            pick_cols = (col_lag == col_shift[t]).astype(jnp.float32).astype(jnp.bfloat16)
            picked = jnp.dot(
                pick_rows, store[owner[t], patch[t]], preferred_element_type=jnp.float32
            )
            moved = jnp.dot(
                picked.astype(jnp.bfloat16), pick_cols, preferred_element_type=jnp.float32
            )
            first = pl.multiple_of(t * TS, TS)
            template_ref[:, pl.ds(first, TS)] = (before + moved[:, :TS]).astype(jnp.bfloat16)
            before = moved[:, TS:]
        return before

    last = lax.fori_loop(0, tiles // per_step, cut, jnp.zeros((TS, TS), jnp.float32))
    template_ref[:, tiles * TS :] = last.astype(jnp.bfloat16)

    def rim_copy(source, landing, which, step):
        return pltpu.make_async_remote_copy(
            src_ref=source,
            dst_ref=landing,
            send_sem=rim_send.at[which],
            recv_sem=rim_recv.at[which],
            device_id=(mine, lax.rem(amp + step, amps)),
            device_id_type=pl.DeviceIdType.MESH,
        )

    onto_next = rim_copy(template_ref.at[pl.ds(rows - RIM, RIM)], top_land, 0, 1)
    onto_previous = rim_copy(template_ref.at[pl.ds(0, RIM)], low_land, 1, amps - 1)
    onto_next.start()
    onto_previous.start()
    own.wait_send()
    for copy in sent:
        copy.wait_send()
    onto_next.wait()
    onto_previous.wait()
    top_ref[...] = jnp.where(amp > 0, top_land[...], jnp.zeros_like(top_land))
    low_ref[...] = jnp.where(amp < amps - 1, low_land[...], jnp.zeros_like(low_land))


def gather_and_cut(ids, coeffs, patches, down, rim_down, pack):
    owners, amps = lax.axis_size("ccd"), lax.axis_size("amp")
    tiles = ids[0].shape[0]
    count, rows, lanes = down.shape
    width = (tiles + 1) * TS
    rim_lanes = -(-count * RIM // TS) * TS
    smem = pl.BlockSpec(memory_space=pltpu.SMEM)
    vmem = pl.BlockSpec(memory_space=pltpu.VMEM)
    chips = owners // 2
    dma = pltpu.SemaphoreType.DMA
    return pl.pallas_call(
        functools.partial(gather_kernel, owners, amps),
        in_specs=[smem] * 5 + [vmem] * 4,
        out_specs=[vmem] * 5,
        out_shape=[
            jax.ShapeDtypeStruct((rows, width), jnp.bfloat16),
            jax.ShapeDtypeStruct((RIM, width), jnp.bfloat16),
            jax.ShapeDtypeStruct((RIM, width), jnp.bfloat16),
            jax.ShapeDtypeStruct((3, rows, count * TS), jnp.bfloat16),
            jax.ShapeDtypeStruct((3, 2 * RIM, rim_lanes), jnp.bfloat16),
        ],
        scratch_shapes=[
            pltpu.VMEM((owners,) + patches.shape, jnp.bfloat16),
            pltpu.VMEM((3, 2 * RIM, count * TS), jnp.bfloat16),
            pltpu.VMEM((RIM, width), jnp.bfloat16),
            pltpu.VMEM((RIM, width), jnp.bfloat16),
            dma((chips - 1, 2)),
            dma((chips - 1, 2)),
            dma((chips - 1, 2)),
            dma((chips - 1, 2)),
            dma(()),
            dma(()),
            dma((2,)),
            dma((2,)),
        ],
        compiler_params=pltpu.CompilerParams(
            collective_id=0, has_side_effects=True, vmem_limit_bytes=VMEM_BYTES
        ),
        cost_estimate=pl.CostEstimate(
            flops=tiles * 2 * TS * 8 * TS * TS, bytes_accessed=6 * 2**20, transcendentals=0
        ),
    )(*ids, coeffs, patches, down, rim_down, pack)


def apply_factors(windows, across_ref, weights, spread, columns, first_column):
    rows = windows[0].shape[0]
    stacked = jnp.concatenate(windows, axis=0)
    for pair in range(across_ref.shape[1] // WINDOW):
        result = jnp.dot(
            stacked,
            across_ref[:, pair * WINDOW : (pair + 1) * WINDOW],
            preferred_element_type=jnp.float32,
        ).astype(jnp.bfloat16)
        for b in range(len(windows)):
            for half in range(2):
                h = 2 * pair + half
                spread[h * rows : (h + 1) * rows, b * TS : (b + 1) * TS] = result[
                    b * rows : (b + 1) * rows, half * TS : (half + 1) * TS
                ]
    filled = across_ref.shape[1] // TS * rows
    if filled < spread.shape[0]:
        spread[filled:, :] = jnp.zeros((spread.shape[0] - filled, spread.shape[1]), spread.dtype)
    folded = jnp.dot(weights, spread[...], preferred_element_type=jnp.float32)
    out_rows = weights.shape[0] // 3
    width = len(windows) * TS
    position = first_column + lax.broadcasted_iota(jnp.int32, (1, width), 1)
    xh = (2.0 * position.astype(jnp.float32) + 1.0) / columns - 1.0
    return folded[:out_rows] + xh * (
        folded[out_rows : 2 * out_rows] + xh * folded[2 * out_rows :]
    )


def centre_kernel(columns, template_ref, across_ref, weight_ref, science_ref, out_ref, spread):
    width = out_ref.shape[1]
    first = pl.program_id(0) * width
    windows = [
        template_ref[:, pl.ds(pl.multiple_of(first + b * TS, TS), WINDOW)]
        for b in range(width // TS)
    ]
    weights = weight_ref[...].reshape(-1, weight_ref.shape[2])
    psf = apply_factors(windows, across_ref, weights, spread, columns, first)
    out_ref[...] = science_ref[...] - psf


def centre(template, across, weights, science, width):
    rows, columns = science.shape
    return pl.pallas_call(
        functools.partial(centre_kernel, columns),
        grid=(columns // width,),
        in_specs=[
            pl.BlockSpec(template.shape, lambda i: (0, 0)),
            pl.BlockSpec(across.shape, lambda i: (0, 0)),
            pl.BlockSpec(weights.shape, lambda i: (0, 0, 0)),
            pl.BlockSpec((rows, width), lambda i: (0, i)),
        ],
        out_specs=pl.BlockSpec((rows, width), lambda i: (0, i)),
        out_shape=jax.ShapeDtypeStruct(science.shape, jnp.float32),
        scratch_shapes=[pltpu.VMEM((weights.shape[2], width), jnp.bfloat16)],
        compiler_params=pltpu.CompilerParams(vmem_limit_bytes=VMEM_BYTES),
        cost_estimate=pl.CostEstimate(
            flops=2 * columns * weights.shape[2] * (3 * rows + WINDOW),
            bytes_accessed=8 * rows * columns + 4 * 2**20,
            transcendentals=0,
        ),
    )(template, across, weights, science)


def rim_kernel(columns, top_ref, low_ref, across_ref, weight_ref, held_ref, out_ref, spread):
    width = out_ref.shape[1]
    first = pl.program_id(1) * width
    is_top = pl.program_id(0) == 0
    windows = []
    for b in range(width // TS):
        where = pl.ds(pl.multiple_of(first + b * TS, TS), WINDOW)
        windows.append(jnp.where(is_top, top_ref[:, where], low_ref[:, where]))
    weights = weight_ref[...].reshape(-1, weight_ref.shape[2])
    psf = apply_factors(windows, across_ref, weights, spread, columns, first)
    out_ref[...] = held_ref[...] - psf


def rims(top, low, across, weights, held, width):
    rows, columns = held.shape
    last = rows // RIM - 1
    return pl.pallas_call(
        functools.partial(rim_kernel, columns),
        grid=(2, columns // width),
        in_specs=[
            pl.BlockSpec(top.shape, lambda v, i: (0, 0)),
            pl.BlockSpec(low.shape, lambda v, i: (0, 0)),
            pl.BlockSpec(across.shape, lambda v, i: (0, 0)),
            pl.BlockSpec((3, RIM, weights.shape[2]), lambda v, i: (0, v, 0)),
            pl.BlockSpec((RIM, width), lambda v, i: (v * last, i)),
        ],
        out_specs=pl.BlockSpec((RIM, width), lambda v, i: (v * last, i)),
        out_shape=jax.ShapeDtypeStruct(held.shape, jnp.float32),
        scratch_shapes=[pltpu.VMEM((weights.shape[2], width), jnp.bfloat16)],
        input_output_aliases={4: 0},
        compiler_params=pltpu.CompilerParams(vmem_limit_bytes=VMEM_BYTES),
        cost_estimate=pl.CostEstimate(
            flops=4 * columns * weights.shape[2] * (3 * RIM + WINDOW),
            bytes_accessed=2**20,
            transcendentals=0,
        ),
    )(top, low, across, weights, held)


def per_device(science, patches, coeffs, tile_owner, tile_patch, tile_offset):
    ccd_id = lax.axis_index("ccd")
    amp_id = lax.axis_index("amp")
    strip_rows, columns = science.shape[1:]

    ids = (
        tile_owner[ccd_id, amp_id, :, 0],
        tile_patch[ccd_id, amp_id],
        tile_offset[ccd_id, amp_id, :, 0],
        tile_offset[ccd_id, amp_id, :, 1],
    )
    across = jnp.asarray(across_matrix())
    row = np.arange(strip_rows)
    down = down_factors(row[None, :] - row[:, None], strip_rows)
    rim_row = np.arange(RIM)
    top_lags = (rim_row[None, :] - RIM) - rim_row[:, None]
    low_lags = (rim_row[None, :] + RIM) - rim_row[:, None]
    rim_down = down_factors(np.concatenate([top_lags, low_lags], axis=0), TS)
    template, top, low, centre_weights, rim_weights = gather_and_cut(
        ids,
        coeffs[0],
        patches[0, 0],
        jnp.asarray(down),
        jnp.asarray(rim_down),
        jnp.asarray(lane_packing()),
    )
    inner = centre(template, across, centre_weights, science[0], 8 * TS)
    return rims(top, low, across, rim_weights, inner, 16 * TS)[None]


def solution(mesh):
    placed = (
        P("ccd", "amp", None),
        P("ccd", "amp", None, None, None),
        P("ccd", None, None),
        P(),
        P(),
        P(),
    )
    return jax.shard_map(
        per_device, mesh=mesh, in_specs=placed, out_specs=P("ccd", "amp", None), check_vma=False
    )
```

```python
import functools

import jax
import jax.numpy as jnp
import ml_dtypes
import numpy as np
from jax import lax
from jax.experimental import pallas as pl
from jax.experimental.pallas import tpu as pltpu
from jax.sharding import PartitionSpec as P

TS = 128
HALF = 10
RIM = 16
WINDOW = 2 * TS
VMEM_BYTES = 60 * 2**20

gauss_widths = (1.0, 2.0, 4.0)
poly_degrees = (4, 4, 3)
poly_powers = ((0, 0), (1, 0), (0, 1), (2, 0), (1, 1), (0, 2))


def factor_table():
    offsets = np.arange(-HALF, HALF + 1).astype(np.float64)
    shapes = []
    for sigma_px, degree in zip(gauss_widths, poly_degrees):
        for exponent in range(degree + 1):
            profile = np.exp(-offsets * offsets / (2.0 * sigma_px * sigma_px))
            profile = profile * (offsets / HALF) ** exponent
            shapes.append(profile / np.sum(np.abs(profile)))
    return np.stack(shapes).astype(np.float32).astype(ml_dtypes.bfloat16).astype(np.float32)


def across_pairs():
    return [(s, p) for s, degree in enumerate(poly_degrees) for p in range(degree + 1)]


def banded(taps, lags):
    inside = np.abs(lags) <= HALF
    return np.where(inside, taps[np.clip(lags + HALF, 0, 2 * HALF)], 0.0)


def across_matrix():
    factors = factor_table()
    lags = np.arange(WINDOW)[:, None] - TS // 2 - np.arange(TS)[None, :]
    return np.concatenate([banded(f, lags) for f in factors], axis=1).astype(ml_dtypes.bfloat16)


def factor_firsts():
    return [int(f) for f in np.concatenate([[0], np.cumsum([d + 1 for d in poly_degrees])])]


def down_factors(lags, lanes):
    bands = np.stack([banded(f, lags) for f in factor_table()])
    return np.pad(bands, ((0, 0), (0, 0), (0, lanes - lags.shape[1]))).astype(ml_dtypes.bfloat16)


def lane_packing():
    pack = np.zeros((TS // RIM, TS, TS))
    for g in range(TS // RIM):
        for r in range(RIM):
            pack[g, r, g * RIM + r] = 1.0
    return pack.reshape(-1, TS).astype(ml_dtypes.bfloat16)


def fold_weights(coeff_ref, yh, down_ref, out_ref):
    firsts = factor_firsts()
    k = 0
    for h, (s, p) in enumerate(across_pairs()):
        count = poly_degrees[s] + 1 - p
        factors = [down_ref[firsts[s] + q].astype(jnp.float32) for q in range(count)]
        terms = [
            sum(coeff_ref[m, 0, k + q] * factors[q] for q in range(count))
            for m in range(len(poly_powers))
        ]
        k += count
        where = slice(h * TS, (h + 1) * TS)
        out_ref[0, :, where] = (terms[0] + yh * (terms[2] + yh * terms[5])).astype(jnp.bfloat16)
        out_ref[1, :, where] = (terms[1] + yh * terms[4]).astype(jnp.bfloat16)
        out_ref[2, :, where] = terms[3].astype(jnp.bfloat16)


def gather_kernel(
    owners,
    amps,
    owner_hbm,
    patch_hbm,
    offset_hbm,
    coeff_hbm,
    patches_hbm,
    down_hbm,
    rim_down_hbm,
    pack_hbm,
    template_ref,
    top_ref,
    low_ref,
    weight_ref,
    rim_weight_ref,
    owner_ref,
    patch_ref,
    offset_ref,
    coeff_ref,
    patches_ref,
    down_ref,
    rim_down_ref,
    pack_ref,
    store,
    rim_wide,
    top_land,
    low_land,
    local_sem,
    direct_send,
    direct_recv,
    relay_send,
    relay_recv,
    pass_send,
    pass_recv,
    own_send,
    own_recv,
    rim_send,
    rim_recv,
):
    mine = lax.axis_index("ccd")
    amp = lax.axis_index("amp")
    core = lax.rem(mine, 2)
    chip = lax.div(mine, 2)
    sibling = chip * 2 + 1 - core
    chips = owners // 2
    half = patches_ref.shape[0] // 2

    fetch_patches = pltpu.make_async_copy(patches_hbm.at[0, 0], patches_ref, local_sem.at[0])
    fetch_patches.start()
    barrier = pltpu.get_barrier_semaphore()
    for step in range(1, owners):
        pl.semaphore_signal(
            barrier,
            inc=1,
            device_id=(lax.rem(mine + step, owners), amp),
            device_id_type=pl.DeviceIdType.MESH,
        )
    for step in (1, amps - 1):
        pl.semaphore_signal(
            barrier,
            inc=1,
            device_id=(mine, lax.rem(amp + step, amps)),
            device_id_type=pl.DeviceIdType.MESH,
        )
    fetches = [
        pltpu.make_async_copy(source, target, local_sem.at[1 + i])
        for i, (source, target) in enumerate(
            (
                (coeff_hbm, coeff_ref),
                (down_hbm, down_ref),
                (rim_down_hbm, rim_down_ref),
                (pack_hbm, pack_ref),
                (owner_hbm.at[mine, amp], owner_ref),
                (patch_hbm.at[mine], patch_ref),
                (offset_hbm.at[mine, amp], offset_ref),
            )
        )
    ]
    for fetch in fetches:
        fetch.start()
    fetch_patches.wait()
    store[mine] = patches_ref[...].astype(jnp.bfloat16)
    pl.semaphore_wait(barrier, owners - 1 + 2)

    def halves(of, which):
        return store.at[of, pl.ds(which * half, half)]

    def move(ref, send_sem, recv_sem, device):
        return pltpu.make_async_remote_copy(
            src_ref=ref,
            dst_ref=ref,
            send_sem=send_sem,
            recv_sem=recv_sem,
            device_id=device,
            device_id_type=pl.DeviceIdType.MESH,
        )

    if chips == 4:
        beside = chip + 1 - 2 * lax.rem(chip, 2)
        above = lax.rem(chip + 2, 4)
        across_both = lax.rem(beside + 2, 4)
        exchanges = [(beside, beside), (above, above)]
    else:
        exchanges = [
            (lax.rem(chip + step, chips), lax.rem(chip + chips - step, chips))
            for step in range(1, chips)
        ]

    sent = []
    for i, (target, _) in enumerate(exchanges):
        for j in range(2):
            copy = move(
                halves(mine, j),
                direct_send.at[i, j],
                direct_recv.at[i, core],
                (target * 2 + j, amp),
            )
            copy.start()
            sent.append(copy)
    own = move(store.at[mine], own_send, own_recv, (sibling, amp))
    own.start()

    for fetch in fetches:
        fetch.wait()
    rows = down_ref.shape[1]
    row = amp * rows + lax.broadcasted_iota(jnp.int32, (rows, 1), 0)
    yh = (2.0 * row.astype(jnp.float32) + 1.0) / (amps * rows) - 1.0
    fold_weights(coeff_ref, yh, down_ref, weight_ref)
    edge = lax.broadcasted_iota(jnp.int32, (2 * RIM, 1), 0)
    edge = amp * rows + jnp.where(edge < RIM, edge, rows - 2 * RIM + edge)
    yh = (2.0 * edge.astype(jnp.float32) + 1.0) / (amps * rows) - 1.0
    fold_weights(coeff_ref, yh, rim_down_ref, rim_wide)
    wide = rim_wide[...].reshape(3 * 2 * RIM, rim_wide.shape[2])
    group = pack_ref.shape[0]
    for g in range(rim_weight_ref.shape[2] // TS):
        part = wide[:, g * group : (g + 1) * group]
        packed = jnp.dot(part, pack_ref[: part.shape[1]], preferred_element_type=jnp.float32)
        rim_weight_ref[:, :, g * TS : (g + 1) * TS] = packed.astype(jnp.bfloat16).reshape(
            3, 2 * RIM, TS
        )

    def pass_on(i, k, source):
        onward = move(
            halves(source * 2 + k, core), pass_send.at[i, k], pass_recv.at[i, k], (sibling, amp)
        )
        onward.start()
        sent.append(onward)

    def relay(which, source, target):
        return move(
            halves(source * 2 + which, core),
            relay_send.at[which],
            relay_recv.at[which],
            (target * 2 + core, amp),
        )

    sources = [source for _, source in exchanges]
    order = [(i, k) for k in range(2) for i in range(len(exchanges))]
    if chips == 4:
        order = [(1, 0), (0, 1), (0, 0), (1, 1)]
    for i, k in order:
        move(
            halves(sources[i] * 2 + k, core),
            direct_send.at[i, k],
            direct_recv.at[i, k],
            (sibling, amp),
        ).wait_recv()
        if chips == 4 and i != k:
            onward = relay(k, sources[i], sources[1 - i])
            onward.start()
            sent.append(onward)
        pass_on(i, k, sources[i])
    if chips == 4:
        for k in range(2):
            relay(k, across_both, beside).wait_recv()
            pass_on(2, k, across_both)
        sources = sources + [across_both]
    move(store.at[sibling], own_send, own_recv, (sibling, amp)).wait_recv()
    for i, source in enumerate(sources):
        for k in range(2):
            move(
                halves(source * 2 + k, 1 - core),
                pass_send.at[i, k],
                pass_recv.at[i, k],
                (sibling, amp),
            ).wait_recv()

    row_lag = lax.broadcasted_iota(jnp.int32, (TS, 2 * TS), 1) - lax.broadcasted_iota(
        jnp.int32, (TS, 2 * TS), 0
    )
    col_lag = lax.broadcasted_iota(jnp.int32, (2 * TS, 2 * TS), 0) - lax.broadcasted_iota(
        jnp.int32, (2 * TS, 2 * TS), 1
    )
    column = lax.broadcasted_iota(jnp.int32, (2 * TS, 2 * TS), 1)
    held = (column >= TS // 2) & (column < TS // 2 + TS)
    col_lag = jnp.where(held, col_lag + TS // 2, -1)
    tiles = owner_ref.shape[1]
    per_step = 8

    def cut(step, before):
        for j in range(per_step):
            t = step * per_step + j
            pick_rows = (row_lag == offset_ref[0, t]).astype(jnp.float32).astype(jnp.bfloat16)
            pick_cols = (col_lag == offset_ref[1, t]).astype(jnp.float32).astype(jnp.bfloat16)
            picked = jnp.dot(
                pick_rows, store[owner_ref[0, t], patch_ref[amp, t]], preferred_element_type=jnp.float32
            )
            moved = jnp.dot(
                picked.astype(jnp.bfloat16), pick_cols, preferred_element_type=jnp.float32
            )
            first = pl.multiple_of(t * TS, TS)
            template_ref[:, pl.ds(first, TS)] = (before + moved[:, :TS]).astype(jnp.bfloat16)
            before = moved[:, TS:]
        return before

    def rim_copies(part, where):
        return [
            pltpu.make_async_remote_copy(
                src_ref=template_ref.at[pl.ds(first, RIM), where],
                dst_ref=landing.at[:, where],
                send_sem=rim_send.at[part, which],
                recv_sem=rim_recv.at[part, which],
                device_id=(mine, lax.rem(amp + step, amps)),
                device_id_type=pl.DeviceIdType.MESH,
            )
            for which, (first, landing, step) in enumerate(
                ((rows - RIM, top_land, 1), (0, low_land, amps - 1))
            )
        ]

    steps = tiles // per_step
    early = steps // 2 * per_step * TS
    before = lax.fori_loop(0, steps // 2, cut, jnp.zeros((TS, TS), jnp.float32))
    rims = rim_copies(0, pl.ds(0, early))
    for copy in rims:
        copy.start()
    last = lax.fori_loop(steps // 2, steps, cut, before)
    template_ref[:, tiles * TS :] = last.astype(jnp.bfloat16)
    rest = rim_copies(1, pl.ds(early, (tiles + 1) * TS - early))
    for copy in rest:
        copy.start()
    own.wait_send()
    for copy in sent:
        copy.wait_send()
    for copy in rims + rest:
        copy.wait()
    top_ref[...] = jnp.where(amp > 0, top_land[...], jnp.zeros_like(top_land))
    low_ref[...] = jnp.where(amp < amps - 1, low_land[...], jnp.zeros_like(low_land))


def gather_and_cut(owner, patch, offset, coeffs, patches, down, rim_down, pack):
    owners, amps = lax.axis_size("ccd"), lax.axis_size("amp")
    tiles = patch.shape[2]
    count, rows, lanes = down.shape
    width = (tiles + 1) * TS
    rim_lanes = -(-count * RIM // TS) * TS
    vmem = pl.BlockSpec(memory_space=pltpu.VMEM)
    chips = owners // 2
    dma = pltpu.SemaphoreType.DMA
    return pl.pallas_call(
        functools.partial(gather_kernel, owners, amps),
        in_specs=[pl.BlockSpec(memory_space=pl.ANY)] * 8,
        out_specs=[vmem] * 5,
        out_shape=[
            jax.ShapeDtypeStruct((rows, width), jnp.bfloat16),
            jax.ShapeDtypeStruct((RIM, width), jnp.bfloat16),
            jax.ShapeDtypeStruct((RIM, width), jnp.bfloat16),
            jax.ShapeDtypeStruct((3, rows, count * TS), jnp.bfloat16),
            jax.ShapeDtypeStruct((3, 2 * RIM, rim_lanes), jnp.bfloat16),
        ],
        scratch_shapes=[
            pltpu.SMEM(owner.shape[2:], jnp.int32),
            pltpu.SMEM(patch.shape[1:], jnp.int32),
            pltpu.SMEM(offset.shape[2:], jnp.int32),
            pltpu.SMEM(coeffs.shape, jnp.float32),
            pltpu.VMEM(patches.shape[2:], jnp.float32),
            pltpu.VMEM(down.shape, jnp.bfloat16),
            pltpu.VMEM(rim_down.shape, jnp.bfloat16),
            pltpu.VMEM(pack.shape, jnp.bfloat16),
            pltpu.VMEM((owners,) + patches.shape[2:], jnp.bfloat16),
            pltpu.VMEM((3, 2 * RIM, count * TS), jnp.bfloat16),
            pltpu.VMEM((RIM, width), jnp.bfloat16),
            pltpu.VMEM((RIM, width), jnp.bfloat16),
            dma((8,)),
            dma((chips - 1, 2)),
            dma((chips - 1, 2)),
            dma((2,)),
            dma((2,)),
            dma((chips - 1, 2)),
            dma((chips - 1, 2)),
            dma(()),
            dma(()),
            dma((2, 2)),
            dma((2, 2)),
        ],
        compiler_params=pltpu.CompilerParams(
            collective_id=0, has_side_effects=True, vmem_limit_bytes=VMEM_BYTES
        ),
        cost_estimate=pl.CostEstimate(
            flops=tiles * 2 * TS * 8 * TS * TS, bytes_accessed=6 * 2**20, transcendentals=0
        ),
    )(owner, patch, offset, coeffs, patches, down, rim_down, pack)


def polynomial(folded, xh):
    rows = folded.shape[0] // 3
    return folded[:rows] + xh * (folded[rows : 2 * rows] + xh * folded[2 * rows :])


def filter_kernel(
    columns,
    template_ref,
    top_ref,
    low_ref,
    across_ref,
    weight_ref,
    rim_weight_ref,
    science_ref,
    out_ref,
    spread,
    rim_spread,
):
    rows, width = out_ref.shape
    blocks = width // TS
    first = pl.program_id(0) * width
    starts = [pl.multiple_of(first + b * TS, TS) for b in range(blocks)]
    parts = [(template_ref, spread, rows), (top_ref, rim_spread.at[0], RIM)]
    parts.append((low_ref, rim_spread.at[1], RIM))
    stacked = jnp.concatenate(
        [ref[:, pl.ds(start, WINDOW)] for ref, _, _ in parts for start in starts], axis=0
    )
    for pair in range(across_ref.shape[1] // WINDOW):
        result = jnp.dot(
            stacked,
            across_ref[:, pair * WINDOW : (pair + 1) * WINDOW],
            preferred_element_type=jnp.float32,
        ).astype(jnp.bfloat16)
        begin = 0
        for _, target, height in parts:
            for b in range(blocks):
                for side in range(2):
                    h = 2 * pair + side
                    target[h * height : (h + 1) * height, b * TS : (b + 1) * TS] = result[
                        begin : begin + height, side * TS : (side + 1) * TS
                    ]
                begin += height
    filled = across_ref.shape[1] // TS * RIM
    if filled < rim_spread.shape[1]:
        unused = (2, rim_spread.shape[1] - filled, width)
        rim_spread[:, filled:, :] = jnp.zeros(unused, rim_spread.dtype)
    position = first + lax.broadcasted_iota(jnp.int32, (1, width), 1)
    xh = (2.0 * position.astype(jnp.float32) + 1.0) / columns - 1.0
    weights = weight_ref[...].reshape(3 * rows, weight_ref.shape[2])
    folded = jnp.dot(weights, spread[...], preferred_element_type=jnp.float32)
    out_ref[...] = science_ref[...] - polynomial(folded, xh)
    for side, begin in enumerate((0, rows - RIM)):
        weights = rim_weight_ref[:, side * RIM : (side + 1) * RIM, :]
        weights = weights.reshape(3 * RIM, rim_weight_ref.shape[2])
        folded = jnp.dot(weights, rim_spread[side], preferred_element_type=jnp.float32)
        out_ref[begin : begin + RIM, :] -= polynomial(folded, xh)


def filter_strip(template, top, low, across, weights, rim_weights, science, width):
    rows, columns = science.shape

    def whole(array):
        return pl.BlockSpec(array.shape, lambda i: (0,) * array.ndim)

    constant = (template, top, low, across, weights, rim_weights)
    return pl.pallas_call(
        functools.partial(filter_kernel, columns),
        grid=(columns // width,),
        in_specs=[whole(x) for x in constant] + [pl.BlockSpec((rows, width), lambda i: (0, i))],
        out_specs=pl.BlockSpec((rows, width), lambda i: (0, i)),
        out_shape=jax.ShapeDtypeStruct(science.shape, jnp.float32),
        scratch_shapes=[
            pltpu.VMEM((weights.shape[2], width), jnp.bfloat16),
            pltpu.VMEM((2, rim_weights.shape[2], width), jnp.bfloat16),
        ],
        compiler_params=pltpu.CompilerParams(vmem_limit_bytes=VMEM_BYTES),
        cost_estimate=pl.CostEstimate(
            flops=2 * columns * weights.shape[2] * (3 * rows + WINDOW),
            bytes_accessed=8 * rows * columns + 4 * 2**20,
            transcendentals=0,
        ),
    )(*constant, science)


def per_device(science, patches, coeffs, tile_owner, tile_patch, tile_offset):
    strip_rows = science.shape[1]

    across = jnp.asarray(across_matrix())
    row = np.arange(strip_rows)
    down = down_factors(row[None, :] - row[:, None], strip_rows)
    rim_row = np.arange(RIM)
    top_lags = (rim_row[None, :] - RIM) - rim_row[:, None]
    low_lags = (rim_row[None, :] + RIM) - rim_row[:, None]
    rim_down = down_factors(np.concatenate([top_lags, low_lags], axis=0), TS)
    template, top, low, weights, rim_weights = gather_and_cut(
        jnp.transpose(tile_owner, (0, 1, 3, 2)),
        tile_patch,
        jnp.transpose(tile_offset, (0, 1, 3, 2)),
        jnp.transpose(coeffs, (2, 0, 1)),
        patches,
        jnp.asarray(down),
        jnp.asarray(rim_down),
        jnp.asarray(lane_packing()),
    )
    return filter_strip(
        template, top, low, across, weights, rim_weights, science[0], 8 * TS
    )[None]


def solution(mesh):
    placed = (
        P("ccd", "amp", None),
        P("ccd", "amp", None, None, None),
        P("ccd", None, None),
        P(),
        P(),
        P(),
    )
    return jax.shard_map(
        per_device, mesh=mesh, in_specs=placed, out_specs=P("ccd", "amp", None), check_vma=False
    )
```

```python
import functools

import jax
import jax.numpy as jnp
import ml_dtypes
import numpy as np
from jax import lax
from jax.experimental import pallas as pl
from jax.experimental.pallas import tpu as pltpu
from jax.sharding import PartitionSpec as P

TS = 128
HALF = 10
RIM = 16
WINDOW = 2 * TS
VMEM_BYTES = 60 * 2**20

gauss_widths = (1.0, 2.0, 4.0)
poly_degrees = (4, 4, 3)
poly_powers = ((0, 0), (1, 0), (0, 1), (2, 0), (1, 1), (0, 2))


def factor_table():
    offsets = np.arange(-HALF, HALF + 1).astype(np.float64)
    shapes = []
    for sigma_px, degree in zip(gauss_widths, poly_degrees):
        for exponent in range(degree + 1):
            profile = np.exp(-offsets * offsets / (2.0 * sigma_px * sigma_px))
            profile = profile * (offsets / HALF) ** exponent
            shapes.append(profile / np.sum(np.abs(profile)))
    return np.stack(shapes).astype(np.float32).astype(ml_dtypes.bfloat16).astype(np.float32)


def across_pairs():
    return [(s, p) for s, degree in enumerate(poly_degrees) for p in range(degree + 1)]


def banded(taps, lags):
    inside = np.abs(lags) <= HALF
    return np.where(inside, taps[np.clip(lags + HALF, 0, 2 * HALF)], 0.0)


def across_matrix():
    factors = factor_table()
    lags = np.arange(WINDOW)[:, None] - TS // 2 - np.arange(TS)[None, :]
    return np.concatenate([banded(f, lags) for f in factors], axis=1).astype(ml_dtypes.bfloat16)


def factor_firsts():
    return [int(f) for f in np.concatenate([[0], np.cumsum([d + 1 for d in poly_degrees])])]


def down_factors(lags, lanes):
    bands = np.stack([banded(f, lags) for f in factor_table()])
    return np.pad(bands, ((0, 0), (0, 0), (0, lanes - lags.shape[1]))).astype(ml_dtypes.bfloat16)


def lane_packing():
    pack = np.zeros((TS // RIM, TS, TS))
    for g in range(TS // RIM):
        for r in range(RIM):
            pack[g, r, g * RIM + r] = 1.0
    return pack.reshape(-1, TS).astype(ml_dtypes.bfloat16)


def fold_weights(coeff_ref, yh, down_ref, out_ref):
    firsts = factor_firsts()
    k = 0
    for h, (s, p) in enumerate(across_pairs()):
        count = poly_degrees[s] + 1 - p
        factors = [down_ref[firsts[s] + q].astype(jnp.float32) for q in range(count)]
        terms = [
            sum(coeff_ref[m, 0, k + q] * factors[q] for q in range(count))
            for m in range(len(poly_powers))
        ]
        k += count
        where = slice(h * TS, (h + 1) * TS)
        out_ref[0, :, where] = (terms[0] + yh * (terms[2] + yh * terms[5])).astype(jnp.bfloat16)
        out_ref[1, :, where] = (terms[1] + yh * terms[4]).astype(jnp.bfloat16)
        out_ref[2, :, where] = terms[3].astype(jnp.bfloat16)


def gather_kernel(
    owners,
    amps,
    owner_hbm,
    patch_hbm,
    offset_hbm,
    coeff_hbm,
    patches_hbm,
    down_hbm,
    rim_down_hbm,
    pack_hbm,
    across_hbm,
    science_hbm,
    out_hbm,
    template_ref,
    weight_ref,
    rim_weight_ref,
    across_ref,
    science_ref,
    result,
    spread,
    rim_spread,
    owner_ref,
    patch_ref,
    offset_ref,
    coeff_ref,
    patches_ref,
    down_ref,
    rim_down_ref,
    pack_ref,
    store,
    rim_wide,
    top_land,
    low_land,
    local_sem,
    out_sem,
    direct_send,
    direct_recv,
    relay_send,
    relay_recv,
    pass_send,
    pass_recv,
    own_send,
    own_recv,
    rim_send,
    rim_recv,
):
    mine = lax.axis_index("ccd")
    amp = lax.axis_index("amp")
    core = lax.rem(mine, 2)
    chip = lax.div(mine, 2)
    sibling = chip * 2 + 1 - core
    chips = owners // 2
    half = patches_ref.shape[0] // 2

    fetch_patches = pltpu.make_async_copy(patches_hbm.at[0, 0], patches_ref, local_sem.at[0])
    fetch_patches.start()
    barrier = pltpu.get_barrier_semaphore()
    for step in range(1, owners):
        pl.semaphore_signal(
            barrier,
            inc=1,
            device_id=(lax.rem(mine + step, owners), amp),
            device_id_type=pl.DeviceIdType.MESH,
        )
    for step in (1, amps - 1):
        pl.semaphore_signal(
            barrier,
            inc=1,
            device_id=(mine, lax.rem(amp + step, amps)),
            device_id_type=pl.DeviceIdType.MESH,
        )
    fetches = [
        pltpu.make_async_copy(source, target, local_sem.at[1 + i])
        for i, (source, target) in enumerate(
            (
                (coeff_hbm, coeff_ref),
                (down_hbm, down_ref),
                (rim_down_hbm, rim_down_ref),
                (pack_hbm, pack_ref),
                (owner_hbm.at[mine, amp], owner_ref),
                (patch_hbm.at[mine], patch_ref),
                (offset_hbm.at[mine, amp], offset_ref),
                (across_hbm, across_ref),
                (science_hbm.at[0], science_ref),
            )
        )
    ]
    for fetch in fetches:
        fetch.start()
    fetch_patches.wait()
    store[mine] = patches_ref[...].astype(jnp.bfloat16)
    pl.semaphore_wait(barrier, owners - 1 + 2)

    def halves(of, which):
        return store.at[of, pl.ds(which * half, half)]

    def move(ref, send_sem, recv_sem, device):
        return pltpu.make_async_remote_copy(
            src_ref=ref,
            dst_ref=ref,
            send_sem=send_sem,
            recv_sem=recv_sem,
            device_id=device,
            device_id_type=pl.DeviceIdType.MESH,
        )

    if chips == 4:
        beside = chip + 1 - 2 * lax.rem(chip, 2)
        above = lax.rem(chip + 2, 4)
        across_both = lax.rem(beside + 2, 4)
        exchanges = [(beside, beside), (above, above)]
    else:
        exchanges = [
            (lax.rem(chip + step, chips), lax.rem(chip + chips - step, chips))
            for step in range(1, chips)
        ]

    sent = []
    for i, (target, _) in enumerate(exchanges):
        for j in range(2):
            copy = move(
                halves(mine, j),
                direct_send.at[i, j],
                direct_recv.at[i, core],
                (target * 2 + j, amp),
            )
            copy.start()
            sent.append(copy)
    own = move(store.at[mine], own_send, own_recv, (sibling, amp))
    own.start()

    for fetch in fetches:
        fetch.wait()
    rows = down_ref.shape[1]
    row = amp * rows + lax.broadcasted_iota(jnp.int32, (rows, 1), 0)
    yh = (2.0 * row.astype(jnp.float32) + 1.0) / (amps * rows) - 1.0
    fold_weights(coeff_ref, yh, down_ref, weight_ref)
    edge = lax.broadcasted_iota(jnp.int32, (2 * RIM, 1), 0)
    edge = amp * rows + jnp.where(edge < RIM, edge, rows - 2 * RIM + edge)
    yh = (2.0 * edge.astype(jnp.float32) + 1.0) / (amps * rows) - 1.0
    fold_weights(coeff_ref, yh, rim_down_ref, rim_wide)
    wide = rim_wide[...].reshape(3 * 2 * RIM, rim_wide.shape[2])
    group = pack_ref.shape[0]
    for g in range(rim_weight_ref.shape[2] // TS):
        part = wide[:, g * group : (g + 1) * group]
        packed = jnp.dot(part, pack_ref[: part.shape[1]], preferred_element_type=jnp.float32)
        rim_weight_ref[:, :, g * TS : (g + 1) * TS] = packed.astype(jnp.bfloat16).reshape(
            3, 2 * RIM, TS
        )

    def pass_on(i, k, source):
        onward = move(
            halves(source * 2 + k, core), pass_send.at[i, k], pass_recv.at[i, k], (sibling, amp)
        )
        onward.start()
        sent.append(onward)

    def relay(which, source, target):
        return move(
            halves(source * 2 + which, core),
            relay_send.at[which],
            relay_recv.at[which],
            (target * 2 + core, amp),
        )

    sources = [source for _, source in exchanges]
    order = [(i, k) for k in range(2) for i in range(len(exchanges))]
    if chips == 4:
        order = [(1, 0), (0, 1), (0, 0), (1, 1)]
    for i, k in order:
        move(
            halves(sources[i] * 2 + k, core),
            direct_send.at[i, k],
            direct_recv.at[i, k],
            (sibling, amp),
        ).wait_recv()
        if chips == 4 and i != k:
            onward = relay(k, sources[i], sources[1 - i])
            onward.start()
            sent.append(onward)
        pass_on(i, k, sources[i])
    if chips == 4:
        for k in range(2):
            relay(k, across_both, beside).wait_recv()
            pass_on(2, k, across_both)
        sources = sources + [across_both]
    move(store.at[sibling], own_send, own_recv, (sibling, amp)).wait_recv()
    for i, source in enumerate(sources):
        for k in range(2):
            move(
                halves(source * 2 + k, 1 - core),
                pass_send.at[i, k],
                pass_recv.at[i, k],
                (sibling, amp),
            ).wait_recv()

    row_lag = lax.broadcasted_iota(jnp.int32, (TS, 2 * TS), 1) - lax.broadcasted_iota(
        jnp.int32, (TS, 2 * TS), 0
    )
    col_lag = lax.broadcasted_iota(jnp.int32, (2 * TS, 2 * TS), 0) - lax.broadcasted_iota(
        jnp.int32, (2 * TS, 2 * TS), 1
    )
    column = lax.broadcasted_iota(jnp.int32, (2 * TS, 2 * TS), 1)
    held = (column >= TS // 2) & (column < TS // 2 + TS)
    col_lag = jnp.where(held, col_lag + TS // 2, -1)
    tiles = owner_ref.shape[1]
    per_step = 8

    def cut(step, before):
        for j in range(per_step):
            t = step * per_step + j
            pick_rows = (row_lag == offset_ref[0, t]).astype(jnp.float32).astype(jnp.bfloat16)
            pick_cols = (col_lag == offset_ref[1, t]).astype(jnp.float32).astype(jnp.bfloat16)
            picked = jnp.dot(
                pick_rows, store[owner_ref[0, t], patch_ref[amp, t]], preferred_element_type=jnp.float32
            )
            moved = jnp.dot(
                picked.astype(jnp.bfloat16), pick_cols, preferred_element_type=jnp.float32
            )
            first = pl.multiple_of(t * TS, TS)
            template_ref[:, pl.ds(first, TS)] = (before + moved[:, :TS]).astype(jnp.bfloat16)
            before = moved[:, TS:]
        return before

    def rim_copies(part, where):
        return [
            pltpu.make_async_remote_copy(
                src_ref=template_ref.at[pl.ds(first, RIM), where],
                dst_ref=landing.at[:, where],
                send_sem=rim_send.at[part, which],
                recv_sem=rim_recv.at[part, which],
                device_id=(mine, lax.rem(amp + step, amps)),
                device_id_type=pl.DeviceIdType.MESH,
            )
            for which, (first, landing, step) in enumerate(
                ((rows - RIM, top_land, 1), (0, low_land, amps - 1))
            )
        ]

    steps = tiles // per_step
    early = steps // 2 * per_step * TS
    before = lax.fori_loop(0, steps // 2, cut, jnp.zeros((TS, TS), jnp.float32))
    rims = rim_copies(0, pl.ds(0, early))
    for copy in rims:
        copy.start()
    last = lax.fori_loop(steps // 2, steps, cut, before)
    template_ref[:, tiles * TS :] = last.astype(jnp.bfloat16)
    rest = rim_copies(1, pl.ds(early, (tiles + 1) * TS - early))
    for copy in rest:
        copy.start()
    def receive(copies, where):
        for copy in copies:
            copy.wait()
        blank = jnp.zeros((RIM, where.stop - where.start), jnp.bfloat16)
        top_land[:, where] = jnp.where(amp > 0, top_land[:, where], blank)
        low_land[:, where] = jnp.where(amp < amps - 1, low_land[:, where], blank)

    receive(rims, slice(0, early))
    columns = science_ref.shape[1]
    width = spread.shape[1]

    def result_copy(i):
        where = pl.ds(pl.multiple_of(i * width, width), width)
        return pltpu.make_async_copy(
            result.at[:, where], out_hbm.at[0, :, where], out_sem.at[i]
        )

    def chunk(i, carried):
        @pl.when(i == 1)
        def _():
            receive(rest, slice(early, (tiles + 1) * TS))

        filter_chunk(
            columns,
            i * width,
            template_ref,
            top_land,
            low_land,
            across_ref,
            weight_ref,
            rim_weight_ref,
            science_ref,
            result,
            spread,
            rim_spread,
        )
        result_copy(i).start()
        return carried

    lax.fori_loop(0, columns // width, chunk, 0)
    own.wait_send()
    for copy in sent:
        copy.wait_send()
    for i in range(columns // width):
        result_copy(i).wait()


def gather_and_cut(owner, patch, offset, coeffs, patches, down, rim_down, pack, across, science, chunk_width):
    owners, amps = lax.axis_size("ccd"), lax.axis_size("amp")
    tiles = patch.shape[2]
    count, rows, lanes = down.shape
    width = (tiles + 1) * TS
    rim_lanes = -(-count * RIM // TS) * TS
    strip = science.shape[1:]
    chips = owners // 2
    dma = pltpu.SemaphoreType.DMA
    return pl.pallas_call(
        functools.partial(gather_kernel, owners, amps),
        in_specs=[pl.BlockSpec(memory_space=pl.ANY)] * 10,
        out_specs=pl.BlockSpec(memory_space=pl.ANY),
        out_shape=jax.ShapeDtypeStruct(science.shape, jnp.float32),
        scratch_shapes=[
            pltpu.VMEM((rows, width), jnp.bfloat16),
            pltpu.VMEM((3, rows, count * TS), jnp.bfloat16),
            pltpu.VMEM((3, 2 * RIM, rim_lanes), jnp.bfloat16),
            pltpu.VMEM(across.shape, jnp.bfloat16),
            pltpu.VMEM(strip, jnp.float32),
            pltpu.VMEM(strip, jnp.float32),
            pltpu.VMEM((count * TS, chunk_width), jnp.bfloat16),
            pltpu.VMEM((2, rim_lanes, chunk_width), jnp.bfloat16),
            pltpu.SMEM(owner.shape[2:], jnp.int32),
            pltpu.SMEM(patch.shape[1:], jnp.int32),
            pltpu.SMEM(offset.shape[2:], jnp.int32),
            pltpu.SMEM(coeffs.shape, jnp.float32),
            pltpu.VMEM(patches.shape[2:], jnp.float32),
            pltpu.VMEM(down.shape, jnp.bfloat16),
            pltpu.VMEM(rim_down.shape, jnp.bfloat16),
            pltpu.VMEM(pack.shape, jnp.bfloat16),
            pltpu.VMEM((owners,) + patches.shape[2:], jnp.bfloat16),
            pltpu.VMEM((3, 2 * RIM, count * TS), jnp.bfloat16),
            pltpu.VMEM((RIM, width), jnp.bfloat16),
            pltpu.VMEM((RIM, width), jnp.bfloat16),
            dma((10,)),
            dma((strip[1] // chunk_width,)),
            dma((chips - 1, 2)),
            dma((chips - 1, 2)),
            dma((2,)),
            dma((2,)),
            dma((chips - 1, 2)),
            dma((chips - 1, 2)),
            dma(()),
            dma(()),
            dma((2, 2)),
            dma((2, 2)),
        ],
        compiler_params=pltpu.CompilerParams(
            collective_id=0, has_side_effects=True, vmem_limit_bytes=VMEM_BYTES
        ),
        cost_estimate=pl.CostEstimate(
            flops=2 * strip[1] * count * TS * (3 * rows + WINDOW), bytes_accessed=10 * 2**20, transcendentals=0
        ),
    )(owner, patch, offset, coeffs, patches, down, rim_down, pack, across, science)


def polynomial(folded, xh):
    rows = folded.shape[0] // 3
    return folded[:rows] + xh * (folded[rows : 2 * rows] + xh * folded[2 * rows :])


def filter_chunk(
    columns,
    first,
    template_ref,
    top_ref,
    low_ref,
    across_ref,
    weight_ref,
    rim_weight_ref,
    science_ref,
    out_ref,
    spread,
    rim_spread,
):
    rows, width = out_ref.shape[0], spread.shape[1]
    blocks = width // TS
    here = pl.ds(pl.multiple_of(first, width), width)
    starts = [pl.multiple_of(first + b * TS, TS) for b in range(blocks)]
    parts = [(template_ref, spread, rows), (top_ref, rim_spread.at[0], RIM)]
    parts.append((low_ref, rim_spread.at[1], RIM))
    stacked = jnp.concatenate(
        [ref[:, pl.ds(start, WINDOW)] for ref, _, _ in parts for start in starts], axis=0
    )
    for pair in range(across_ref.shape[1] // WINDOW):
        result = jnp.dot(
            stacked,
            across_ref[:, pair * WINDOW : (pair + 1) * WINDOW],
            preferred_element_type=jnp.float32,
        ).astype(jnp.bfloat16)
        begin = 0
        for _, target, height in parts:
            for b in range(blocks):
                for side in range(2):
                    h = 2 * pair + side
                    target[h * height : (h + 1) * height, b * TS : (b + 1) * TS] = result[
                        begin : begin + height, side * TS : (side + 1) * TS
                    ]
                begin += height
    filled = across_ref.shape[1] // TS * RIM
    if filled < rim_spread.shape[1]:
        unused = (2, rim_spread.shape[1] - filled, width)
        rim_spread[:, filled:, :] = jnp.zeros(unused, rim_spread.dtype)
    position = first + lax.broadcasted_iota(jnp.int32, (1, width), 1)
    xh = (2.0 * position.astype(jnp.float32) + 1.0) / columns - 1.0
    weights = weight_ref[...].reshape(3 * rows, weight_ref.shape[2])
    folded = jnp.dot(weights, spread[...], preferred_element_type=jnp.float32)
    out_ref[:, here] = science_ref[:, here] - polynomial(folded, xh)
    for side, begin in enumerate((0, rows - RIM)):
        weights = rim_weight_ref[:, side * RIM : (side + 1) * RIM, :]
        weights = weights.reshape(3 * RIM, rim_weight_ref.shape[2])
        folded = jnp.dot(weights, rim_spread[side], preferred_element_type=jnp.float32)
        out_ref[begin : begin + RIM, here] -= polynomial(folded, xh)


def per_device(science, patches, coeffs, tile_owner, tile_patch, tile_offset):
    strip_rows = science.shape[1]

    across = jnp.asarray(across_matrix())
    row = np.arange(strip_rows)
    down = down_factors(row[None, :] - row[:, None], strip_rows)
    rim_row = np.arange(RIM)
    top_lags = (rim_row[None, :] - RIM) - rim_row[:, None]
    low_lags = (rim_row[None, :] + RIM) - rim_row[:, None]
    rim_down = down_factors(np.concatenate([top_lags, low_lags], axis=0), TS)
    return gather_and_cut(
        jnp.transpose(tile_owner, (0, 1, 3, 2)),
        tile_patch,
        jnp.transpose(tile_offset, (0, 1, 3, 2)),
        jnp.transpose(coeffs, (2, 0, 1)),
        patches,
        jnp.asarray(down),
        jnp.asarray(rim_down),
        jnp.asarray(lane_packing()),
        across,
        science,
        8 * TS,
    )


def solution(mesh):
    placed = (
        P("ccd", "amp", None),
        P("ccd", "amp", None, None, None),
        P("ccd", None, None),
        P(),
        P(),
        P(),
    )
    return jax.shard_map(
        per_device, mesh=mesh, in_specs=placed, out_specs=P("ccd", "amp", None), check_vma=False
    )
```

```python
import functools

import jax
import jax.numpy as jnp
import ml_dtypes
import numpy as np
from jax import lax
from jax.experimental import pallas as pl
from jax.experimental.pallas import tpu as pltpu
from jax.sharding import PartitionSpec as P

TS = 128
HALF = 10
RIM = 16
WINDOW = 2 * TS
VMEM_BYTES = 60 * 2**20

gauss_widths = (1.0, 2.0, 4.0)
poly_degrees = (4, 4, 3)
poly_powers = ((0, 0), (1, 0), (0, 1), (2, 0), (1, 1), (0, 2))


def factor_table():
    offsets = np.arange(-HALF, HALF + 1).astype(np.float64)
    shapes = []
    for sigma_px, degree in zip(gauss_widths, poly_degrees):
        for exponent in range(degree + 1):
            profile = np.exp(-offsets * offsets / (2.0 * sigma_px * sigma_px))
            profile = profile * (offsets / HALF) ** exponent
            shapes.append(profile / np.sum(np.abs(profile)))
    return np.stack(shapes).astype(np.float32).astype(ml_dtypes.bfloat16).astype(np.float32)


def across_pairs():
    return [(s, p) for s, degree in enumerate(poly_degrees) for p in range(degree + 1)]


def banded(taps, lags):
    inside = np.abs(lags) <= HALF
    return np.where(inside, taps[np.clip(lags + HALF, 0, 2 * HALF)], 0.0)


def across_matrix():
    factors = factor_table()
    lags = np.arange(WINDOW)[:, None] - TS // 2 - np.arange(TS)[None, :]
    return np.concatenate([banded(f, lags) for f in factors], axis=1).astype(ml_dtypes.bfloat16)


def factor_firsts():
    return [int(f) for f in np.concatenate([[0], np.cumsum([d + 1 for d in poly_degrees])])]


def down_factors(lags, lanes):
    bands = np.stack([banded(f, lags) for f in factor_table()])
    return np.pad(bands, ((0, 0), (0, 0), (0, lanes - lags.shape[1]))).astype(ml_dtypes.bfloat16)


def lane_packing():
    pack = np.zeros((TS // RIM, TS, TS))
    for g in range(TS // RIM):
        for r in range(RIM):
            pack[g, r, g * RIM + r] = 1.0
    return pack.reshape(-1, TS).astype(ml_dtypes.bfloat16)


def fold_weights(coeff_ref, yh, down_ref, out_ref):
    firsts = factor_firsts()
    k = 0
    for h, (s, p) in enumerate(across_pairs()):
        count = poly_degrees[s] + 1 - p
        factors = [down_ref[firsts[s] + q].astype(jnp.float32) for q in range(count)]
        terms = [
            sum(coeff_ref[m, 0, k + q] * factors[q] for q in range(count))
            for m in range(len(poly_powers))
        ]
        k += count
        where = slice(h * TS, (h + 1) * TS)
        out_ref[0, :, where] = (terms[0] + yh * (terms[2] + yh * terms[5])).astype(jnp.bfloat16)
        out_ref[1, :, where] = (terms[1] + yh * terms[4]).astype(jnp.bfloat16)
        out_ref[2, :, where] = terms[3].astype(jnp.bfloat16)


def gather_kernel(
    owners,
    amps,
    owner_hbm,
    patch_hbm,
    offset_hbm,
    coeff_hbm,
    patches_hbm,
    down_hbm,
    rim_down_hbm,
    pack_hbm,
    across_hbm,
    out_hbm,
    template_ref,
    weight_ref,
    rim_weight_ref,
    across_ref,
    result,
    spread,
    rim_spread,
    owner_ref,
    patch_ref,
    offset_ref,
    coeff_ref,
    patches_ref,
    down_ref,
    rim_down_ref,
    pack_ref,
    store,
    rim_wide,
    top_land,
    low_land,
    local_sem,
    out_sem,
    direct_send,
    direct_recv,
    relay_send,
    relay_recv,
    pass_send,
    pass_recv,
    own_send,
    own_recv,
    rim_send,
    rim_recv,
):
    mine = lax.axis_index("ccd")
    amp = lax.axis_index("amp")
    core = lax.rem(mine, 2)
    chip = lax.div(mine, 2)
    sibling = chip * 2 + 1 - core
    chips = owners // 2
    half = patches_ref.shape[0] // 2

    fetch_patches = pltpu.make_async_copy(patches_hbm.at[0, 0], patches_ref, local_sem.at[0])
    fetch_patches.start()
    barrier = pltpu.get_barrier_semaphore()
    for step in range(1, owners):
        pl.semaphore_signal(
            barrier,
            inc=1,
            device_id=(lax.rem(mine + step, owners), amp),
            device_id_type=pl.DeviceIdType.MESH,
        )
    for step in (1, amps - 1):
        pl.semaphore_signal(
            barrier,
            inc=1,
            device_id=(mine, lax.rem(amp + step, amps)),
            device_id_type=pl.DeviceIdType.MESH,
        )
    fetches = [
        pltpu.make_async_copy(source, target, local_sem.at[1 + i])
        for i, (source, target) in enumerate(
            (
                (coeff_hbm, coeff_ref),
                (down_hbm, down_ref),
                (rim_down_hbm, rim_down_ref),
                (pack_hbm, pack_ref),
                (owner_hbm.at[mine, amp], owner_ref),
                (patch_hbm.at[mine], patch_ref),
                (offset_hbm.at[mine, amp], offset_ref),
                (across_hbm, across_ref),
            )
        )
    ]
    for fetch in fetches:
        fetch.start()
    fetch_patches.wait()
    store[mine] = patches_ref[...].astype(jnp.bfloat16)
    pl.semaphore_wait(barrier, owners - 1 + 2)

    def halves(of, which):
        return store.at[of, pl.ds(which * half, half)]

    def move(ref, send_sem, recv_sem, device):
        return pltpu.make_async_remote_copy(
            src_ref=ref,
            dst_ref=ref,
            send_sem=send_sem,
            recv_sem=recv_sem,
            device_id=device,
            device_id_type=pl.DeviceIdType.MESH,
        )

    if chips == 4:
        beside = chip + 1 - 2 * lax.rem(chip, 2)
        above = lax.rem(chip + 2, 4)
        across_both = lax.rem(beside + 2, 4)
        exchanges = [(beside, beside), (above, above)]
    else:
        exchanges = [
            (lax.rem(chip + step, chips), lax.rem(chip + chips - step, chips))
            for step in range(1, chips)
        ]

    sent = []
    for i, (target, _) in enumerate(exchanges):
        for j in range(2):
            copy = move(
                halves(mine, j),
                direct_send.at[i, j],
                direct_recv.at[i, core],
                (target * 2 + j, amp),
            )
            copy.start()
            sent.append(copy)
    own = move(store.at[mine], own_send, own_recv, (sibling, amp))
    own.start()

    for fetch in fetches:
        fetch.wait()
    rows = down_ref.shape[1]
    row = amp * rows + lax.broadcasted_iota(jnp.int32, (rows, 1), 0)
    yh = (2.0 * row.astype(jnp.float32) + 1.0) / (amps * rows) - 1.0
    fold_weights(coeff_ref, yh, down_ref, weight_ref)
    edge = lax.broadcasted_iota(jnp.int32, (2 * RIM, 1), 0)
    edge = amp * rows + jnp.where(edge < RIM, edge, rows - 2 * RIM + edge)
    yh = (2.0 * edge.astype(jnp.float32) + 1.0) / (amps * rows) - 1.0
    fold_weights(coeff_ref, yh, rim_down_ref, rim_wide)
    wide = rim_wide[...].reshape(3 * 2 * RIM, rim_wide.shape[2])
    group = pack_ref.shape[0]
    for g in range(rim_weight_ref.shape[2] // TS):
        part = wide[:, g * group : (g + 1) * group]
        packed = jnp.dot(part, pack_ref[: part.shape[1]], preferred_element_type=jnp.float32)
        rim_weight_ref[:, :, g * TS : (g + 1) * TS] = packed.astype(jnp.bfloat16).reshape(
            3, 2 * RIM, TS
        )

    def pass_on(i, k, source):
        onward = move(
            halves(source * 2 + k, core), pass_send.at[i, k], pass_recv.at[i, k], (sibling, amp)
        )
        onward.start()
        sent.append(onward)

    def relay(which, source, target):
        return move(
            halves(source * 2 + which, core),
            relay_send.at[which],
            relay_recv.at[which],
            (target * 2 + core, amp),
        )

    sources = [source for _, source in exchanges]
    order = [(i, k) for k in range(2) for i in range(len(exchanges))]
    if chips == 4:
        order = [(1, 0), (0, 1), (0, 0), (1, 1)]
    for i, k in order:
        move(
            halves(sources[i] * 2 + k, core),
            direct_send.at[i, k],
            direct_recv.at[i, k],
            (sibling, amp),
        ).wait_recv()
        if chips == 4 and i != k:
            onward = relay(k, sources[i], sources[1 - i])
            onward.start()
            sent.append(onward)
        pass_on(i, k, sources[i])
    if chips == 4:
        for k in range(2):
            relay(k, across_both, beside).wait_recv()
            pass_on(2, k, across_both)
        sources = sources + [across_both]
    move(store.at[sibling], own_send, own_recv, (sibling, amp)).wait_recv()
    for i, source in enumerate(sources):
        for k in range(2):
            move(
                halves(source * 2 + k, 1 - core),
                pass_send.at[i, k],
                pass_recv.at[i, k],
                (sibling, amp),
            ).wait_recv()

    row_lag = lax.broadcasted_iota(jnp.int32, (TS, 2 * TS), 1) - lax.broadcasted_iota(
        jnp.int32, (TS, 2 * TS), 0
    )
    col_lag = lax.broadcasted_iota(jnp.int32, (2 * TS, 2 * TS), 0) - lax.broadcasted_iota(
        jnp.int32, (2 * TS, 2 * TS), 1
    )
    column = lax.broadcasted_iota(jnp.int32, (2 * TS, 2 * TS), 1)
    held = (column >= TS // 2) & (column < TS // 2 + TS)
    col_lag = jnp.where(held, col_lag + TS // 2, -1)
    tiles = owner_ref.shape[1]
    per_step = 8

    def cut(step, before):
        for j in range(per_step):
            t = step * per_step + j
            pick_rows = (row_lag == offset_ref[0, t]).astype(jnp.float32).astype(jnp.bfloat16)
            pick_cols = (col_lag == offset_ref[1, t]).astype(jnp.float32).astype(jnp.bfloat16)
            picked = jnp.dot(
                pick_rows, store[owner_ref[0, t], patch_ref[amp, t]], preferred_element_type=jnp.float32
            )
            moved = jnp.dot(
                picked.astype(jnp.bfloat16), pick_cols, preferred_element_type=jnp.float32
            )
            first = pl.multiple_of(t * TS, TS)
            template_ref[:, pl.ds(first, TS)] = (before + moved[:, :TS]).astype(jnp.bfloat16)
            before = moved[:, TS:]
        return before

    def rim_copies(part, where):
        return [
            pltpu.make_async_remote_copy(
                src_ref=template_ref.at[pl.ds(first, RIM), where],
                dst_ref=landing.at[:, where],
                send_sem=rim_send.at[part, which],
                recv_sem=rim_recv.at[part, which],
                device_id=(mine, lax.rem(amp + step, amps)),
                device_id_type=pl.DeviceIdType.MESH,
            )
            for which, (first, landing, step) in enumerate(
                ((rows - RIM, top_land, 1), (0, low_land, amps - 1))
            )
        ]

    steps = tiles // per_step
    early = steps // 2 * per_step * TS
    before = lax.fori_loop(0, steps // 2, cut, jnp.zeros((TS, TS), jnp.float32))
    rims = rim_copies(0, pl.ds(0, early))
    for copy in rims:
        copy.start()
    last = lax.fori_loop(steps // 2, steps, cut, before)
    template_ref[:, tiles * TS :] = last.astype(jnp.bfloat16)
    rest = rim_copies(1, pl.ds(early, (tiles + 1) * TS - early))
    for copy in rest:
        copy.start()
    def receive(copies, where):
        for copy in copies:
            copy.wait()
        blank = jnp.zeros((RIM, where.stop - where.start), jnp.bfloat16)
        top_land[:, where] = jnp.where(amp > 0, top_land[:, where], blank)
        low_land[:, where] = jnp.where(amp < amps - 1, low_land[:, where], blank)

    receive(rims, slice(0, early))
    columns = result.shape[1]
    width = spread.shape[1]

    def result_copy(i):
        where = pl.ds(pl.multiple_of(i * width, width), width)
        return pltpu.make_async_copy(
            result.at[:, where], out_hbm.at[0, :, where], out_sem.at[i]
        )

    def chunk(i, carried):
        @pl.when(i == 1)
        def _():
            receive(rest, slice(early, (tiles + 1) * TS))

        filter_chunk(
            columns,
            i * width,
            template_ref,
            top_land,
            low_land,
            across_ref,
            weight_ref,
            rim_weight_ref,
            result,
            spread,
            rim_spread,
        )
        result_copy(i).start()
        return carried

    lax.fori_loop(0, columns // width, chunk, 0)
    own.wait_send()
    for copy in sent:
        copy.wait_send()
    for i in range(columns // width):
        result_copy(i).wait()


def gather_and_cut(owner, patch, offset, coeffs, patches, down, rim_down, pack, across, science, chunk_width):
    owners, amps = lax.axis_size("ccd"), lax.axis_size("amp")
    tiles = patch.shape[2]
    count, rows, lanes = down.shape
    width = (tiles + 1) * TS
    rim_lanes = -(-count * RIM // TS) * TS
    strip = science.shape[1:]
    chips = owners // 2
    dma = pltpu.SemaphoreType.DMA
    return pl.pallas_call(
        functools.partial(gather_kernel, owners, amps),
        in_specs=[pl.BlockSpec(memory_space=pl.ANY)] * 9,
        out_specs=pl.BlockSpec(memory_space=pl.ANY),
        out_shape=jax.ShapeDtypeStruct(science.shape, jnp.float32),
        scratch_shapes=[
            pltpu.VMEM((rows, width), jnp.bfloat16),
            pltpu.VMEM((3, rows, count * TS), jnp.bfloat16),
            pltpu.VMEM((3, 2 * RIM, rim_lanes), jnp.bfloat16),
            pltpu.VMEM(across.shape, jnp.bfloat16),
            pltpu.VMEM(strip, jnp.float32),
            pltpu.VMEM((count * TS, chunk_width), jnp.bfloat16),
            pltpu.VMEM((2, rim_lanes, chunk_width), jnp.bfloat16),
            pltpu.SMEM(owner.shape[2:], jnp.int32),
            pltpu.SMEM(patch.shape[1:], jnp.int32),
            pltpu.SMEM(offset.shape[2:], jnp.int32),
            pltpu.SMEM(coeffs.shape, jnp.float32),
            pltpu.VMEM(patches.shape[2:], jnp.float32),
            pltpu.VMEM(down.shape, jnp.bfloat16),
            pltpu.VMEM(rim_down.shape, jnp.bfloat16),
            pltpu.VMEM(pack.shape, jnp.bfloat16),
            pltpu.VMEM((owners,) + patches.shape[2:], jnp.bfloat16),
            pltpu.VMEM((3, 2 * RIM, count * TS), jnp.bfloat16),
            pltpu.VMEM((RIM, width), jnp.bfloat16),
            pltpu.VMEM((RIM, width), jnp.bfloat16),
            dma((10,)),
            dma((strip[1] // chunk_width,)),
            dma((chips - 1, 2)),
            dma((chips - 1, 2)),
            dma((2,)),
            dma((2,)),
            dma((chips - 1, 2)),
            dma((chips - 1, 2)),
            dma(()),
            dma(()),
            dma((2, 2)),
            dma((2, 2)),
        ],
        compiler_params=pltpu.CompilerParams(
            collective_id=0, has_side_effects=True, vmem_limit_bytes=VMEM_BYTES
        ),
        cost_estimate=pl.CostEstimate(
            flops=2 * strip[1] * count * TS * (3 * rows + WINDOW), bytes_accessed=10 * 2**20, transcendentals=0
        ),
    )(owner, patch, offset, coeffs, patches, down, rim_down, pack, across)


def polynomial(folded, xh):
    rows = folded.shape[0] // 3
    return folded[:rows] + xh * (folded[rows : 2 * rows] + xh * folded[2 * rows :])


def filter_chunk(
    columns,
    first,
    template_ref,
    top_ref,
    low_ref,
    across_ref,
    weight_ref,
    rim_weight_ref,
    out_ref,
    spread,
    rim_spread,
):
    rows, width = out_ref.shape[0], spread.shape[1]
    blocks = width // TS
    here = pl.ds(pl.multiple_of(first, width), width)
    starts = [pl.multiple_of(first + b * TS, TS) for b in range(blocks)]
    parts = [(template_ref, spread, rows), (top_ref, rim_spread.at[0], RIM)]
    parts.append((low_ref, rim_spread.at[1], RIM))
    stacked = jnp.concatenate(
        [ref[:, pl.ds(start, WINDOW)] for ref, _, _ in parts for start in starts], axis=0
    )
    for pair in range(across_ref.shape[1] // WINDOW):
        result = jnp.dot(
            stacked,
            across_ref[:, pair * WINDOW : (pair + 1) * WINDOW],
            preferred_element_type=jnp.float32,
        ).astype(jnp.bfloat16)
        begin = 0
        for _, target, height in parts:
            for b in range(blocks):
                for side in range(2):
                    h = 2 * pair + side
                    target[h * height : (h + 1) * height, b * TS : (b + 1) * TS] = result[
                        begin : begin + height, side * TS : (side + 1) * TS
                    ]
                begin += height
    filled = across_ref.shape[1] // TS * RIM
    if filled < rim_spread.shape[1]:
        unused = (2, rim_spread.shape[1] - filled, width)
        rim_spread[:, filled:, :] = jnp.zeros(unused, rim_spread.dtype)
    position = first + lax.broadcasted_iota(jnp.int32, (1, width), 1)
    xh = (2.0 * position.astype(jnp.float32) + 1.0) / columns - 1.0
    weights = weight_ref[...].reshape(3 * rows, weight_ref.shape[2])
    folded = jnp.dot(weights, spread[...], preferred_element_type=jnp.float32)
    out_ref[:, here] = polynomial(folded, xh)
    for side, begin in enumerate((0, rows - RIM)):
        weights = rim_weight_ref[:, side * RIM : (side + 1) * RIM, :]
        weights = weights.reshape(3 * RIM, rim_weight_ref.shape[2])
        folded = jnp.dot(weights, rim_spread[side], preferred_element_type=jnp.float32)
        out_ref[begin : begin + RIM, here] += polynomial(folded, xh)


def per_device(science, patches, coeffs, tile_owner, tile_patch, tile_offset):
    strip_rows = science.shape[1]

    across = jnp.asarray(across_matrix())
    row = np.arange(strip_rows)
    down = down_factors(row[None, :] - row[:, None], strip_rows)
    rim_row = np.arange(RIM)
    top_lags = (rim_row[None, :] - RIM) - rim_row[:, None]
    low_lags = (rim_row[None, :] + RIM) - rim_row[:, None]
    rim_down = down_factors(np.concatenate([top_lags, low_lags], axis=0), TS)
    psf_model = gather_and_cut(
        jnp.transpose(tile_owner, (0, 1, 3, 2)),
        tile_patch,
        jnp.transpose(tile_offset, (0, 1, 3, 2)),
        jnp.transpose(coeffs, (2, 0, 1)),
        patches,
        jnp.asarray(down),
        jnp.asarray(rim_down),
        jnp.asarray(lane_packing()),
        across,
        science,
        8 * TS,
    )
    return science - psf_model


def solution(mesh):
    placed = (
        P("ccd", "amp", None),
        P("ccd", "amp", None, None, None),
        P("ccd", None, None),
        P(),
        P(),
        P(),
    )
    return jax.shard_map(
        per_device, mesh=mesh, in_specs=placed, out_specs=P("ccd", "amp", None), check_vma=False
    )
```
